512 devices in a mesh: tile: 64 (over x, z, y_lo), orient: 8 (over y_hi, core).
Axes of the slice: x: 4, y: 8 (y_hi: 4, y_lo: 2; y = y_hi * 2 + y_lo), z: 8, core: 2. Of those that a mesh axis runs over, the one named last changes fastest.
Arguments:
- micrographs: bfloat16 [64, 512, 512], P('tile'), may hold values from -6 to 6
- templates: bfloat16 [64, 8, 256, 256], P('tile', 'orient'), may hold values from -0.0234375 to 0.0234375
- quarter_turns: int32 [64, 8], P('tile', 'orient'), may hold values from 0 to 3
- plan: int32 [64], replicated, may hold values from 0 to 63, each once
Outputs:
- best_score: float32 [64, 512, 512], P('tile', 'orient')
- mean_score: float32 [64, 512, 512], P('tile', 'orient')
The draws below stay inside these ranges and needn't reach their ends.
Inputs may be any that keep to these rules, and one draw needn't show every extreme that they name: `plan`: every tile index appears exactly once; the steps use the first 2 entries.
All inputs are finite; a program needn't handle non-finite values.
Results may differ from the reference program's by a relative error of at most 0.018.
Values may be sent and summed in bfloat16 or wider, within the bound.
A program may use at most 64 MiB of HBM per device.

```python
import jax
import jax.numpy as jnp
from jax import lax

SIDE = 512
TEMPLATE_SIDE = 256
STEPS = 2
BLOCK = 1
TILES = 64
N_TILE = 64
N_ORIENT = 8


def with_ends(drawn, rng, smallest, largest):
    dims = drawn.shape
    spot = [jax.random.randint(jax.random.fold_in(rng, axis), (), 0, dims[axis]) for axis in range(len(dims))]
    drawn = drawn.at[tuple(spot)].set(smallest)
    longest = dims.index(max(dims))
    spot[longest] = (spot[longest] + 1) % dims[longest]
    return drawn.at[tuple(spot)].set(largest)


def steps_of(stream_key, shape, shards, least, high):
    factor_of = 1.0
    for dim, parts in shards:
        heights = jax.random.uniform(jax.random.fold_in(jax.random.fold_in(stream_key, 6), dim), (parts,), jnp.float32, least / len(shards), high / len(shards))
        factor_of = factor_of * jnp.repeat(jnp.exp(heights), shape[dim] // parts).reshape((-1,) + (1,) * (len(shape) - 1 - dim))
    return factor_of


def gaussian(key, dims, deviation, reach, split=(), kind=jnp.bfloat16):
    drawn = jax.random.normal(key, dims, jnp.float32) * deviation
    if len(split) > 0:
        drawn = steps_of(key, dims, split, -0.22, 0.18) * drawn
    return jnp.clip(drawn, min=-reach, max=reach).astype(kind)


def setup_inputs(seed: int = 0) -> dict:
    keys = jax.random.split(jax.random.key(seed), 5)
    micrographs = gaussian(keys[0], (TILES, SIDE, SIDE), 1.0, 6.0, ((0, 64),))
    templates = gaussian(keys[1], (N_TILE, N_ORIENT * BLOCK, TEMPLATE_SIDE, TEMPLATE_SIDE), (TEMPLATE_SIDE * TEMPLATE_SIDE) ** -0.5, 0.0234375, ((0, 64), (1, 8)))
    quarter_turns = with_ends(jax.random.randint(keys[2], (N_TILE, N_ORIENT * BLOCK), 0, 4), jax.random.fold_in(keys[2], 1), 0, 3).astype(jnp.int32)
    plan = jax.random.permutation(keys[3], N_TILE).astype(jnp.int32)
    return dict(micrographs=micrographs, templates=templates, quarter_turns=quarter_turns, plan=plan)


def dft_tables(length):
    positions = jnp.arange(length, dtype=jnp.int32)
    phase_index = (positions[:, None] * positions[None, :]) % length
    angles = (2.0 * jnp.pi / length) * phase_index.astype(jnp.float32)
    return jnp.cos(angles).astype(jnp.bfloat16), jnp.sin(angles).astype(jnp.bfloat16)


def spectrum(pixels, cosine_table, sine_table):
    extent = pixels.shape[-1]
    part_re = jnp.dot(cosine_table[:, :extent], pixels, preferred_element_type=jnp.float32).astype(jnp.bfloat16)
    part_im = (-jnp.dot(sine_table[:, :extent], pixels, preferred_element_type=jnp.float32)).astype(jnp.bfloat16)
    right_cos = cosine_table[:extent, :]
    right_sin = sine_table[:extent, :]
    spec_re = jnp.dot(part_re, right_cos, preferred_element_type=jnp.float32) + jnp.dot(part_im, right_sin, preferred_element_type=jnp.float32)
    spec_im = jnp.dot(part_im, right_cos, preferred_element_type=jnp.float32) - jnp.dot(part_re, right_sin, preferred_element_type=jnp.float32)
    return spec_re.astype(jnp.bfloat16), spec_im.astype(jnp.bfloat16)


def rotate(pixels, quarter):
    options = [pixels, jnp.rot90(pixels, 1), jnp.rot90(pixels, 2), jnp.rot90(pixels, 3)]
    result = options[0]
    for turn_count in range(1, 4):
        result = jnp.where(quarter == turn_count, options[turn_count], result)
    return result


def correlate(spec_re, spec_im, tmpl_re, tmpl_im, cosine_table, sine_table):
    length = spec_re.shape[-1]
    x_re = spec_re.astype(jnp.float32)
    x_im = spec_im.astype(jnp.float32)
    t_re = tmpl_re.astype(jnp.float32)
    t_im = tmpl_im.astype(jnp.float32)
    prod_re = (x_re * t_re + x_im * t_im).astype(jnp.bfloat16)
    prod_im = (x_im * t_re - x_re * t_im).astype(jnp.bfloat16)
    mid_re = (jnp.dot(prod_re, cosine_table, preferred_element_type=jnp.float32) - jnp.dot(prod_im, sine_table, preferred_element_type=jnp.float32)).astype(jnp.bfloat16)
    mid_im = (jnp.dot(prod_re, sine_table, preferred_element_type=jnp.float32) + jnp.dot(prod_im, cosine_table, preferred_element_type=jnp.float32)).astype(jnp.bfloat16)
    scores = jnp.dot(cosine_table, mid_re, preferred_element_type=jnp.float32) - jnp.dot(sine_table, mid_im, preferred_element_type=jnp.float32)
    return scores / float(length * length)


def reference(micrographs, templates, quarter_turns, plan):
    cosine_table, sine_table = dft_tables(SIDE)
    searched = STEPS * N_ORIENT * BLOCK
    owners = plan[:STEPS].astype(jnp.int32)
    chosen = templates[owners].reshape(searched, TEMPLATE_SIDE, TEMPLATE_SIDE)
    quarters = quarter_turns[owners].reshape(searched)

    def template_spectrum(members):
        return spectrum(rotate(members[0], members[1]), cosine_table, sine_table)

    tmpl_re, tmpl_im = lax.map(template_spectrum, (chosen, quarters))

    def per_tile(pixels):
        spec_re, spec_im = spectrum(pixels, cosine_table, sine_table)

        def add_template(carried, spectra_pair):
            best_score, running_sum = carried
            scores = correlate(spec_re, spec_im, spectra_pair[0], spectra_pair[1], cosine_table, sine_table)
            return (jnp.maximum(best_score, scores), running_sum + scores), None

        initial = (jnp.full((SIDE, SIDE), -jnp.inf, dtype=jnp.float32), jnp.zeros((SIDE, SIDE), jnp.float32))
        (best_score, running_sum), _ = lax.scan(add_template, initial, (tmpl_re, tmpl_im))
        return best_score, running_sum / float(searched)

    best_score, mean_score = lax.map(per_tile, micrographs)
    return best_score, mean_score
```

```python
import functools

import jax
import jax.numpy as jnp
import numpy as np
from jax import lax
from jax.experimental import pallas as pl
from jax.experimental.pallas import tpu as pltpu
from jax.sharding import PartitionSpec as P

MESH = pl.DeviceIdType.MESH
BF = jnp.bfloat16
F32 = jnp.float32
SIDE = 512
SEARCHED = 16


def radix_tables():
    j = np.arange(128)
    forward = []
    for r in range(4):
        phase = (np.outer(4 * j + r, j) % SIDE).astype(np.float32)
        angle = np.float32(2.0 * np.pi / SIDE) * phase
        c, s = np.cos(angle), np.sin(angle)
        forward.append(np.block([[c, s], [-s, c]]))
    forward = np.stack(forward).astype(np.float32)
    return forward.astype(jnp.bfloat16), forward.transpose(0, 2, 1).astype(jnp.bfloat16)


def coords():
    tile = lax.axis_index("tile")
    orient = lax.axis_index("orient")
    x, z = lax.div(tile, 16), lax.rem(lax.div(tile, 2), 8)
    y = lax.div(orient, 2) * 2 + lax.rem(tile, 2)
    return x, z, y, lax.rem(orient, 2)


def device(x, z, y, core):
    return (x * 16 + z * 2 + lax.rem(y, 2), lax.div(y, 2) * 2 + core)


def remote(src, dst, send, recv, target):
    return pltpu.make_async_remote_copy(
        src_ref=src, dst_ref=dst, send_sem=send, recv_sem=recv, device_id=target, device_id_type=MESH
    )


def dot(a, b):
    return jnp.dot(a, b, preferred_element_type=F32)


def rotate(block, quarter):
    turns = jnp.full((256, 256), quarter, jnp.int32)
    row = lax.broadcasted_iota(jnp.int32, (256, 256), 0)
    col = lax.broadcasted_iota(jnp.int32, (256, 256), 1)
    same = (row == col).astype(F32)
    swapped = (row + col == 255).astype(F32)
    flip_rows = jnp.where((turns == 1) | (turns == 2), swapped, same).astype(BF)
    flip_cols = jnp.where((turns == 2) | (turns == 3), swapped, same).astype(BF)
    wide = block.astype(F32)
    turned = jnp.where((turns == 1) | (turns == 3), wide.T, wide).astype(BF)
    return dot(dot(flip_rows, turned).astype(BF), flip_cols).astype(BF)


def tile_spectrum(mic, fwd, fwd_t, work, spec):
    quarters = [mic[0, 128 * q : 128 * q + 128, :].astype(F32) for q in range(4)]
    a, b = quarters[0] + quarters[2], quarters[1] + quarters[3]
    c, d = quarters[0] - quarters[2], quarters[1] - quarters[3]
    outs = [
        dot(fwd[0, :, :128], (a + b).astype(BF)),
        dot(fwd[1], jnp.concatenate([c, -d], axis=0).astype(BF)),
        dot(fwd[2, :, :128], (a - b).astype(BF)),
        dot(fwd[3], jnp.concatenate([c, d], axis=0).astype(BF)),
    ]
    for r1 in range(4):
        re = [outs[r1][:128, 128 * p : 128 * p + 128] for p in range(4)]
        im = [outs[r1][128:, 128 * p : 128 * p + 128] for p in range(4)]
        rows = pl.ds(128 * r1, 128)
        rs, rd, im_s, im_d = re[0] + re[2], re[0] - re[2], im[0] + im[2], im[0] - im[2]
        ro, rp, io, ip = re[1] + re[3], re[1] - re[3], im[1] + im[3], im[1] - im[3]
        pairs = [(rs + ro, im_s + io), (rd + ip, im_d - rp), (rs - ro, im_s - io), (rd - ip, im_d + rp)]
        for r2, (p_re, p_im) in enumerate(pairs):
            work[r2, rows, :128] = p_re.astype(BF)
            work[r2, rows, 128:] = p_im.astype(BF)
    for r2 in range(4):
        spec[r2] = dot(work[r2], fwd_t[r2]).astype(BF)


def inverse_rows(fwd_t, quarter, left):
    for r in range(4):
        turn = lax.rem(quarter * r, 4)
        turn = jnp.full((128, 128), turn, jnp.int32)
        c = fwd_t[r, :128, :128].astype(F32)
        s = fwd_t[r, 128:, :128].astype(F32)
        new_c = jnp.where(turn == 0, c, jnp.where(turn == 1, -s, jnp.where(turn == 2, -c, s))).astype(BF)
        new_s = jnp.where(turn == 0, s, jnp.where(turn == 1, c, jnp.where(turn == 2, -s, -c)))
        left[:128, 256 * r : 256 * r + 128] = new_c
        left[128:, 256 * r + 128 : 256 * r + 256] = new_c
        left[:128, 256 * r + 128 : 256 * r + 256] = (-new_s).astype(BF)
        left[128:, 256 * r : 256 * r + 128] = new_s.astype(BF)


def pair_scores(block, fwd, fwd_t, spec, left, work, prod, best, total, first):
    a0, a1 = [jnp.concatenate([block(q, 0, 0), block(q, 1, 0)], axis=1).astype(F32) for q in range(2)]
    b0, b1 = [jnp.concatenate([block(q, 0, 1), block(q, 1, 1)], axis=1).astype(F32) for q in range(2)]
    stacked = [(a0 + a1, b0 + b1), (a0 + b1, b0 - a1), (a0 - a1, b0 - b1), (a0 - b1, b0 + a1)]
    for r1 in range(4):
        out = dot(fwd[r1], jnp.concatenate(stacked[r1], axis=0).astype(BF))
        re0, re1, im0, im1 = out[:128, :128], out[:128, 128:], out[128:, :128], out[128:, 128:]
        rows = pl.ds(128 * r1, 128)
        pairs = [(re0 + re1, im0 + im1), (re0 + im1, im0 - re1), (re0 - re1, im0 - im1), (re0 - im1, im0 + re1)]
        for r2, (p_re, p_im) in enumerate(pairs):
            work[r2, rows, :128] = p_re.astype(BF)
            work[r2, rows, 128:] = p_im.astype(BF)
    for r2 in range(4):
        found = dot(work[r2], fwd_t[r2])
        t_re, t_im = found[:, :128].astype(BF).astype(F32), found[:, 128:].astype(BF).astype(F32)
        x_re, x_im = spec[r2, :, :128].astype(F32), spec[r2, :, 128:].astype(F32)
        p_re = (x_re * t_re + x_im * t_im).astype(BF)
        p_im = (x_im * t_re - x_re * t_im).astype(BF)
        lanes = pl.ds(128 * r2, 128)
        for r1 in range(4):
            prod[pl.ds(256 * r1, 128), lanes] = p_re[128 * r1 : 128 * r1 + 128]
            prod[pl.ds(256 * r1 + 128, 128), lanes] = p_im[128 * r1 : 128 * r1 + 128]
    mid = dot(left[...], prod[...]).astype(BF)
    u = []
    for r2 in range(4):
        lanes = slice(128 * r2, 128 * r2 + 128)
        u.append(dot(jnp.concatenate([mid[:128, lanes], mid[128:, lanes]], axis=1), fwd[r2]))
    re = [v[:, :128] for v in u]
    im = [v[:, 128:] for v in u]
    rs, rd, im_s, im_d = re[0] + re[2], re[0] - re[2], im[0] + im[2], im[0] - im[2]
    ro, rp, io, ip = re[1] + re[3], re[1] - re[3], im[1] + im[3], im[1] - im[3]
    one = [rs + ro, rd - ip, rs - ro, rd + ip]
    two = [-(im_s + io), -(im_d + rp), io - im_s, rp - im_d]
    for q in range(4):
        lanes = pl.ds(128 * q, 128)
        top, both = jnp.maximum(one[q], two[q]), one[q] + two[q]
        if first:
            best[:, lanes] = top
            total[:, lanes] = both
        else:
            best[:, lanes] = jnp.maximum(best[:, lanes], top)
            total[:, lanes] = total[:, lanes] + both


def kernel(
    quarter, plan, mic, tmpl, fwd, fwd_t, best_out, mean_out,
    turned, got, line, tx, tz, spec, work, prod, left, best, total, give, take,
    a_send, a_recv, y_send, y_recv, sx_send, sx_recv, sz_send, sz_recv, bx_send, bx_recv, bz_send, bz_recv, c_send, c_recv,
):
    x, z, y, core = coords()
    around = [(dx, dz) for dx in range(4) for dz in range(8) if (dx, dz) != (0, 0)]
    plane = [(lax.rem(x + dx, 4), lax.rem(z + dz, 8)) for dx, dz in around]
    x_peers = [device(lax.rem(x + d, 4), z, y, core) for d in range(1, 4)]
    z_peers = [device(x, lax.rem(z + d, 8), y, core) for d in range(1, 8)]
    y_peers = [device(x, z, lax.rem(y + d, 8), core) for d in range(1, 8)]
    other = device(x, z, y, 1 - core)

    barrier = pltpu.get_barrier_semaphore()
    greeted = [device(px, pz, y, core) for px, pz in plane] + y_peers + [other]
    for target in greeted:
        pl.semaphore_signal(barrier, inc=1, device_id=target, device_id_type=MESH)

    block = rotate(tmpl[0, 0], quarter[0, 0])
    for q in range(2):
        for h in range(2):
            turned[pl.ds(16 * q + 8 * h, 8)] = block[128 * q : 128 * q + 128, 128 * h : 128 * h + 128].reshape(8, 16, 128)
    tile_spectrum(mic, fwd, fwd_t, work, spec)
    inverse_rows(fwd_t, lax.div(y, 2), left)
    pl.semaphore_wait(barrier, len(greeted))

    mine = x * 8 + z
    sends = []
    for i, (px, pz) in enumerate(plane):
        copy = remote(turned.at[px * 8 + pz], got.at[mine], a_send.at[i], a_recv.at[i], device(px, pz, y, core))
        copy.start()
        sends.append(copy)
    got[mine] = turned[mine]
    for copy in sends:
        copy.wait_recv()

    owners = [plan[s] for s in range(2)]
    for s in range(2):
        line[y, s] = got[lax.div(owners[s], 2)]
    y_copies = []
    for i, target in enumerate(y_peers):
        copy = remote(line.at[y], line.at[y], y_send.at[i], y_recv.at[i], target)
        copy.start()
        y_copies.append(copy)
    for copy in y_copies:
        copy.wait_recv()
    sends += y_copies

    for s in range(2):
        low = lax.rem(owners[s], 2)
        tz[z, x, s] = line[low, s]
        for p in range(3):
            tx[x, p, z, s] = line[2 * (p + 1) + low, s]
    z_copies = [
        remote(tx.at[x, :, z], tx.at[x, :, z], sz_send.at[i], sz_recv.at[i], target) for i, target in enumerate(z_peers)
    ]
    x_copies = [
        remote(tz.at[z, x], tz.at[z, x], sx_send.at[i], sx_recv.at[i], target) for i, target in enumerate(x_peers)
    ]
    for copy in z_copies + x_copies:
        copy.start()
    for copy in x_copies:
        copy.wait_recv()
    last_z = [remote(tz.at[z], tz.at[z], bz_send.at[i], bz_recv.at[i], target) for i, target in enumerate(z_peers)]
    for copy in last_z:
        copy.start()
    for copy in z_copies:
        copy.wait_recv()
    last_x = []
    for p in range(3):
        group = []
        for i, target in enumerate(x_peers):
            copy = remote(tx.at[x, p], tx.at[x, p], bx_send.at[p, i], bx_recv.at[p, i], target)
            copy.start()
            group.append(copy)
        last_x.append(group)
    sends += z_copies + x_copies + last_z

    def from_x(p):
        return lambda q, h, s: tx[2 * q + h, p, :, s].reshape(128, 128)

    def from_z(q, h, s):
        return tz[:, 2 * q + h, s].reshape(128, 128)

    for copy in last_x[0]:
        copy.wait_recv()
    pair_scores(from_x(0), fwd, fwd_t, spec, left, work, prod, best, total, True)
    for copy in last_z:
        copy.wait_recv()
    pair_scores(from_z, fwd, fwd_t, spec, left, work, prod, best, total, False)
    for p in range(1, 3):
        for copy in last_x[p]:
            copy.wait_recv()
        pair_scores(from_x(p), fwd, fwd_t, spec, left, work, prod, best, total, False)

    scale = 1.0 / (SIDE * SIDE)
    theirs, ours = pl.ds((1 - core) * 64, 64), pl.ds(core * 64, 64)
    give[0] = (best[theirs, :] * scale).astype(BF)
    give[1] = (total[theirs, :] * scale).astype(BF)
    swap = remote(give, take, c_send, c_recv, other)
    swap.start()
    swap.wait_recv()
    best_out[0] = jnp.maximum(best[ours, :] * scale, take[0].astype(F32))
    mean_out[0] = (total[ours, :] * scale + take[1].astype(F32)) * (1.0 / SEARCHED)
    swap.wait_send()
    for copy in sends:
        copy.wait_send()
    for group in last_x:
        for copy in group:
            copy.wait_send()


def per_device(micrographs, templates, quarter_turns, plan):
    fwd, fwd_t = radix_tables()
    vmem, smem = pl.BlockSpec(memory_space=pltpu.VMEM), pl.BlockSpec(memory_space=pltpu.SMEM)
    dma = pltpu.SemaphoreType.DMA
    out = jax.ShapeDtypeStruct((1, 64, SIDE), F32)
    return pl.pallas_call(
        kernel,
        out_shape=(out, out),
        in_specs=[smem, smem, vmem, vmem, vmem, vmem],
        out_specs=(vmem, vmem),
        scratch_shapes=[
            pltpu.VMEM((32, 16, 128), BF),
            pltpu.VMEM((32, 16, 128), BF),
            pltpu.VMEM((8, 2, 16, 128), BF),
            pltpu.VMEM((4, 3, 8, 2, 16, 128), BF),
            pltpu.VMEM((8, 4, 2, 16, 128), BF),
            pltpu.VMEM((4, 512, 256), BF),
            pltpu.VMEM((4, 512, 256), BF),
            pltpu.VMEM((1024, 512), BF),
            pltpu.VMEM((256, 1024), BF),
            pltpu.VMEM((128, 512), F32),
            pltpu.VMEM((128, 512), F32),
            pltpu.VMEM((2, 64, 512), BF),
            pltpu.VMEM((2, 64, 512), BF),
            dma((31,)), dma((31,)), dma((7,)), dma((7,)), dma((3,)), dma((3,)), dma((7,)), dma((7,)),
            dma((3, 3)), dma((3, 3)), dma((7,)), dma((7,)), dma(()), dma(()),
        ],
        compiler_params=pltpu.CompilerParams(collective_id=0, has_side_effects=True, vmem_limit_bytes=40 << 20),
        name="match",
    )(quarter_turns, plan, micrographs, templates, jnp.asarray(fwd), jnp.asarray(fwd_t))


def solution(mesh):
    in_specs = (P("tile", None, None), P("tile", "orient", None, None), P("tile", "orient"), P())
    out_specs = (P("tile", "orient", None), P("tile", "orient", None))
    return jax.shard_map(per_device, mesh=mesh, in_specs=in_specs, out_specs=out_specs, check_vma=False)
```

```python
import functools

import jax
import jax.numpy as jnp
import numpy as np
from jax import lax
from jax.experimental import pallas as pl
from jax.experimental.pallas import tpu as pltpu
from jax.sharding import PartitionSpec as P

MESH = pl.DeviceIdType.MESH
BF = jnp.bfloat16
F32 = jnp.float32
SIDE = 512
SEARCHED = 16


def radix_tables():
    j = np.arange(128)
    forward = []
    for r in range(4):
        phase = (np.outer(4 * j + r, j) % SIDE).astype(np.float32)
        angle = np.float32(2.0 * np.pi / SIDE) * phase
        c, s = np.cos(angle), np.sin(angle)
        forward.append(np.block([[c, s], [-s, c]]))
    forward = np.stack(forward).astype(np.float32)
    return forward.astype(jnp.bfloat16), forward.transpose(0, 2, 1).astype(jnp.bfloat16)


def coords():
    tile = lax.axis_index("tile")
    orient = lax.axis_index("orient")
    x, z = lax.div(tile, 16), lax.rem(lax.div(tile, 2), 8)
    y = lax.div(orient, 2) * 2 + lax.rem(tile, 2)
    return x, z, y, lax.rem(orient, 2)


def device(x, z, y, core):
    return (x * 16 + z * 2 + lax.rem(y, 2), lax.div(y, 2) * 2 + core)


def remote(src, dst, send, recv, target):
    return pltpu.make_async_remote_copy(
        src_ref=src, dst_ref=dst, send_sem=send, recv_sem=recv, device_id=target, device_id_type=MESH
    )


def dot(a, b):
    return jnp.dot(a, b, preferred_element_type=F32)


def rotate(block, quarter):
    turns = jnp.full((256, 256), quarter, jnp.int32)
    row = lax.broadcasted_iota(jnp.int32, (256, 256), 0)
    col = lax.broadcasted_iota(jnp.int32, (256, 256), 1)
    same = (row == col).astype(F32)
    swapped = (row + col == 255).astype(F32)
    flip_rows = jnp.where((turns == 1) | (turns == 2), swapped, same).astype(BF)
    flip_cols = jnp.where((turns == 2) | (turns == 3), swapped, same).astype(BF)
    wide = block.astype(F32)
    turned = jnp.where((turns == 1) | (turns == 3), wide.T, wide).astype(BF)
    return dot(dot(flip_rows, turned).astype(BF), flip_cols).astype(BF)


def tile_spectrum(mic, fwd, fwd_t, work, spec):
    quarters = [mic[0, 128 * q : 128 * q + 128, :].astype(F32) for q in range(4)]
    a, b = quarters[0] + quarters[2], quarters[1] + quarters[3]
    c, d = quarters[0] - quarters[2], quarters[1] - quarters[3]
    outs = [
        dot(fwd[0, :, :128], (a + b).astype(BF)),
        dot(fwd[1], jnp.concatenate([c, -d], axis=0).astype(BF)),
        dot(fwd[2, :, :128], (a - b).astype(BF)),
        dot(fwd[3], jnp.concatenate([c, d], axis=0).astype(BF)),
    ]
    for r1 in range(4):
        re = [outs[r1][:128, 128 * p : 128 * p + 128] for p in range(4)]
        im = [outs[r1][128:, 128 * p : 128 * p + 128] for p in range(4)]
        rows = pl.ds(128 * r1, 128)
        rs, rd, im_s, im_d = re[0] + re[2], re[0] - re[2], im[0] + im[2], im[0] - im[2]
        ro, rp, io, ip = re[1] + re[3], re[1] - re[3], im[1] + im[3], im[1] - im[3]
        pairs = [(rs + ro, im_s + io), (rd + ip, im_d - rp), (rs - ro, im_s - io), (rd - ip, im_d + rp)]
        for r2, (p_re, p_im) in enumerate(pairs):
            work[r2, rows, :128] = p_re.astype(BF)
            work[r2, rows, 128:] = p_im.astype(BF)
    for r2 in range(4):
        spec[r2] = dot(work[r2], fwd_t[r2]).astype(BF)


def inverse_rows(fwd_t, quarter, left):
    for r in range(4):
        turn = lax.rem(quarter * r, 4)
        turn = jnp.full((128, 128), turn, jnp.int32)
        c = fwd_t[r, :128, :128].astype(F32)
        s = fwd_t[r, 128:, :128].astype(F32)
        new_c = jnp.where(turn == 0, c, jnp.where(turn == 1, -s, jnp.where(turn == 2, -c, s))).astype(BF)
        new_s = jnp.where(turn == 0, s, jnp.where(turn == 1, c, jnp.where(turn == 2, -s, -c)))
        left[:128, 256 * r : 256 * r + 128] = new_c
        left[128:, 256 * r + 128 : 256 * r + 256] = new_c
        left[:128, 256 * r + 128 : 256 * r + 256] = (-new_s).astype(BF)
        left[128:, 256 * r : 256 * r + 128] = new_s.astype(BF)


def pair_scores(block, fwd, fwd_t, spec, left, work, prod, best, total, first):
    a0, a1 = [jnp.concatenate([block(q, 0, 0), block(q, 1, 0)], axis=1).astype(F32) for q in range(2)]
    b0, b1 = [jnp.concatenate([block(q, 0, 1), block(q, 1, 1)], axis=1).astype(F32) for q in range(2)]
    stacked = [(a0 + a1, b0 + b1), (a0 + b1, b0 - a1), (a0 - a1, b0 - b1), (a0 - b1, b0 + a1)]
    for r1 in range(4):
        out = dot(fwd[r1], jnp.concatenate(stacked[r1], axis=0).astype(BF))
        re0, re1, im0, im1 = out[:128, :128], out[:128, 128:], out[128:, :128], out[128:, 128:]
        rows = pl.ds(128 * r1, 128)
        pairs = [(re0 + re1, im0 + im1), (re0 + im1, im0 - re1), (re0 - re1, im0 - im1), (re0 - im1, im0 + re1)]
        for r2, (p_re, p_im) in enumerate(pairs):
            work[r2, rows, :128] = p_re.astype(BF)
            work[r2, rows, 128:] = p_im.astype(BF)
    for r2 in range(4):
        found = dot(work[r2], fwd_t[r2])
        t_re, t_im = found[:, :128].astype(BF).astype(F32), found[:, 128:].astype(BF).astype(F32)
        x_re, x_im = spec[r2, :, :128].astype(F32), spec[r2, :, 128:].astype(F32)
        p_re = (x_re * t_re + x_im * t_im).astype(BF)
        p_im = (x_im * t_re - x_re * t_im).astype(BF)
        lanes = pl.ds(128 * r2, 128)
        for r1 in range(4):
            prod[pl.ds(256 * r1, 128), lanes] = p_re[128 * r1 : 128 * r1 + 128]
            prod[pl.ds(256 * r1 + 128, 128), lanes] = p_im[128 * r1 : 128 * r1 + 128]
    mid = dot(left[...], prod[...]).astype(BF)
    u = []
    for r2 in range(4):
        lanes = slice(128 * r2, 128 * r2 + 128)
        u.append(dot(jnp.concatenate([mid[:128, lanes], mid[128:, lanes]], axis=1), fwd[r2]))
    re = [v[:, :128] for v in u]
    im = [v[:, 128:] for v in u]
    rs, rd, im_s, im_d = re[0] + re[2], re[0] - re[2], im[0] + im[2], im[0] - im[2]
    ro, rp, io, ip = re[1] + re[3], re[1] - re[3], im[1] + im[3], im[1] - im[3]
    one = [rs + ro, rd - ip, rs - ro, rd + ip]
    two = [-(im_s + io), -(im_d + rp), io - im_s, rp - im_d]
    for q in range(4):
        lanes = pl.ds(128 * q, 128)
        top, both = jnp.maximum(one[q], two[q]), one[q] + two[q]
        if first:
            best[:, lanes] = top
            total[:, lanes] = both
        else:
            best[:, lanes] = jnp.maximum(best[:, lanes], top)
            total[:, lanes] = total[:, lanes] + both


def kernel(
    quarter_in, plan_in, mic_in, tmpl_in, fwd_in, fwd_t_in, out,
    quarter, plan, mic, tmpl, fwd, fwd_t, load, turned, got, line, tx, tz, spec, work, prod, left, best, total, give, take,
    a_send, a_recv, y_send, y_recv, sx_send, sx_recv, sz_send, sz_recv, bx_send, bx_recv, bz_send, bz_recv, c_send, c_recv,
):
    x, z, y, core = coords()

    def hops(dx, dz):
        return min(dx, 4 - dx) + min(dz, 8 - dz)

    around = [(dx, dz) for dx in range(4) for dz in range(8) if (dx, dz) != (0, 0)]
    around.sort(key=lambda step: -hops(*step))
    plane = [(lax.rem(x + dx, 4), lax.rem(z + dz, 8)) for dx, dz in around]
    x_peers = [device(lax.rem(x + d, 4), z, y, core) for d in (2, 1, 3)]
    y_peers = [device(x, z, lax.rem(y + d, 8), core) for d in (4, 3, 5, 2, 6, 1, 7)]
    z_others = [k + (z <= k).astype(jnp.int32) for k in range(7)]
    z_peers = [device(x, other_z, y, core) for other_z in z_others]
    other = device(x, z, y, 1 - core)

    barrier = pltpu.get_barrier_semaphore()
    greeted = [device(px, pz, y, core) for px, pz in plane] + y_peers + [other]
    loads = [
        pltpu.make_async_copy(src, dst, load.at[i])
        for i, (src, dst) in enumerate(
            [(quarter_in, quarter), (tmpl_in, tmpl), (fwd_in, fwd), (mic_in, mic), (fwd_t_in, fwd_t), (plan_in, plan)]
        )
    ]
    for target in greeted:
        pl.semaphore_signal(barrier, inc=1, device_id=target, device_id_type=MESH)
    for copy in loads:
        copy.start()
    loads[0].wait()
    loads[1].wait()

    block = rotate(tmpl[0, 0], quarter[0, 0])
    for q in range(2):
        for h in range(2):
            turned[pl.ds(16 * q + 8 * h, 8)] = block[128 * q : 128 * q + 128, 128 * h : 128 * h + 128].reshape(8, 16, 128)
    pl.semaphore_wait(barrier, len(greeted))

    mine = x * 8 + z
    sends = []
    for i, (px, pz) in enumerate(plane):
        copy = remote(turned.at[px * 8 + pz], got.at[mine], a_send.at[i], a_recv.at[i], device(px, pz, y, core))
        copy.start()
        sends.append(copy)
    got[mine] = turned[mine]
    for copy in loads[2:]:
        copy.wait()
    tile_spectrum(mic, fwd, fwd_t, work, spec)
    inverse_rows(fwd_t, lax.div(y, 2), left)
    for copy in sends:
        copy.wait_recv()

    owners = [plan[s] for s in range(2)]
    for s in range(2):
        line[y, s] = got[lax.div(owners[s], 2)]
    for i, target in enumerate(y_peers):
        copy = remote(line.at[y], line.at[y], y_send.at[i], y_recv.at[y], target)
        copy.start()
        sends.append(copy)

    odd = [jnp.full((16, 128), lax.rem(owners[s], 2), jnp.int32) for s in range(2)]

    def arrived(pair):
        for low in range(2):
            source = 2 * pair + low

            @pl.when(source != y)
            def _():
                remote(line.at[source], line.at[source], y_send.at[0], y_recv.at[source], other).wait_recv()

        return [jnp.where(odd[s] == 0, line[2 * pair, s], line[2 * pair + 1, s]) for s in range(2)]

    own = lax.div(y, 2)
    for s, tile in enumerate(arrived(own)):
        tz[z, x, s] = tile
    x_copies = [
        remote(tz.at[z, x], tz.at[z, x], sx_send.at[i], sx_recv.at[i], target) for i, target in enumerate(x_peers)
    ]
    for copy in x_copies:
        copy.start()
    for p, step in enumerate((1, 3, 2)):
        for s, tile in enumerate(arrived(lax.rem(own + step, 4))):
            tx[x, p, z, s] = tile
        for i, target in enumerate(z_peers):
            copy = remote(tx.at[x, p, z], tx.at[x, p, z], sz_send.at[p, i], sz_recv.at[p, z], target)
            copy.start()
            sends.append(copy)
    for copy in x_copies:
        copy.wait_recv()
    for i, target in enumerate(z_peers):
        copy = remote(tz.at[z], tz.at[z], bz_send.at[i], bz_recv.at[z], target)
        copy.start()
        sends.append(copy)
    last_x = []
    for p in range(3):
        for i, source in enumerate(z_others):
            remote(tx.at[x, p, source], tx.at[x, p, source], sz_send.at[p, i], sz_recv.at[p, source], other).wait_recv()
        group = [
            remote(tx.at[x, p], tx.at[x, p], bx_send.at[p, i], bx_recv.at[p, i], target)
            for i, target in enumerate(x_peers)
        ]
        for copy in group:
            copy.start()
        last_x.append(group)
        sends += group
    sends += x_copies

    def from_x(p):
        return lambda q, h, s: tx[2 * q + h, p, :, s].reshape(128, 128)

    def from_z(q, h, s):
        return tz[:, 2 * q + h, s].reshape(128, 128)

    for copy in last_x[0]:
        copy.wait_recv()
    pair_scores(from_x(0), fwd, fwd_t, spec, left, work, prod, best, total, True)
    for i, source in enumerate(z_others):
        remote(tz.at[source], tz.at[source], bz_send.at[i], bz_recv.at[source], other).wait_recv()
    pair_scores(from_z, fwd, fwd_t, spec, left, work, prod, best, total, False)
    for p in range(1, 3):
        for copy in last_x[p]:
            copy.wait_recv()
        pair_scores(from_x(p), fwd, fwd_t, spec, left, work, prod, best, total, False)

    theirs, ours = pl.ds((1 - core) * 64, 64), pl.ds(core * 64, 64)
    give[0] = best[theirs, :].astype(BF)
    give[1] = total[theirs, :].astype(BF)
    swap = remote(give, take, c_send, c_recv, other)
    swap.start()
    swap.wait_recv()
    out[0] = jnp.maximum(best[ours, :], take[0].astype(F32))
    out[1] = total[ours, :] + take[1].astype(F32)
    swap.wait_send()
    for copy in sends:
        copy.wait_send()


def per_device(micrographs, templates, quarter_turns, plan):
    fwd, fwd_t = radix_tables()
    dma = pltpu.SemaphoreType.DMA
    raw = pl.pallas_call(
        kernel,
        out_shape=jax.ShapeDtypeStruct((2, 64, SIDE), F32),
        in_specs=[pl.BlockSpec(memory_space=pltpu.HBM)] * 6,
        out_specs=pl.BlockSpec(memory_space=pltpu.VMEM),
        scratch_shapes=[
            pltpu.SMEM((1, 1), jnp.int32),
            pltpu.SMEM((64,), jnp.int32),
            pltpu.VMEM((1, SIDE, SIDE), BF),
            pltpu.VMEM((1, 1, 256, 256), BF),
            pltpu.VMEM((4, 256, 256), BF),
            pltpu.VMEM((4, 256, 256), BF),
            dma((6,)),
            pltpu.VMEM((32, 16, 128), BF),
            pltpu.VMEM((32, 16, 128), BF),
            pltpu.VMEM((8, 2, 16, 128), BF),
            pltpu.VMEM((4, 3, 8, 2, 16, 128), BF),
            pltpu.VMEM((8, 4, 2, 16, 128), BF),
            pltpu.VMEM((4, 512, 256), BF),
            pltpu.VMEM((4, 512, 256), BF),
            pltpu.VMEM((1024, 512), BF),
            pltpu.VMEM((256, 1024), BF),
            pltpu.VMEM((128, 512), F32),
            pltpu.VMEM((128, 512), F32),
            pltpu.VMEM((2, 64, 512), BF),
            pltpu.VMEM((2, 64, 512), BF),
            dma((31,)), dma((31,)), dma((7,)), dma((8,)), dma((3,)), dma((3,)), dma((3, 7)), dma((3, 8)),
            dma((3, 3)), dma((3, 3)), dma((7,)), dma((8,)), dma(()), dma(()),
        ],
        compiler_params=pltpu.CompilerParams(collective_id=0, has_side_effects=True, vmem_limit_bytes=107 << 19),
        name="match",
    )(quarter_turns, plan, micrographs, templates, jnp.asarray(fwd), jnp.asarray(fwd_t))
    scale = 1.0 / (SIDE * SIDE)
    return raw[0:1] * scale, raw[1:2] * (scale / SEARCHED)


def solution(mesh):
    in_specs = (P("tile", None, None), P("tile", "orient", None, None), P("tile", "orient"), P())
    out_specs = (P("tile", "orient", None), P("tile", "orient", None))
    return jax.shard_map(per_device, mesh=mesh, in_specs=in_specs, out_specs=out_specs, check_vma=False)
```

```python
import functools

import jax
import jax.numpy as jnp
import numpy as np
from jax import lax
from jax.experimental import pallas as pl
from jax.experimental.pallas import tpu as pltpu
from jax.sharding import PartitionSpec as P

MESH = pl.DeviceIdType.MESH
BF = jnp.bfloat16
F32 = jnp.float32
SIDE = 512
SEARCHED = 16


def radix_tables():
    j = np.arange(128)
    forward = []
    for r in range(4):
        phase = (np.outer(4 * j + r, j) % SIDE).astype(np.float32)
        angle = np.float32(2.0 * np.pi / SIDE) * phase
        c, s = np.cos(angle), np.sin(angle)
        forward.append(np.block([[c, s], [-s, c]]))
    forward = np.stack(forward).astype(np.float32)
    return forward.astype(jnp.bfloat16), forward.transpose(0, 2, 1).astype(jnp.bfloat16)


def coords():
    tile = lax.axis_index("tile")
    orient = lax.axis_index("orient")
    x, z = lax.div(tile, 16), lax.rem(lax.div(tile, 2), 8)
    y = lax.div(orient, 2) * 2 + lax.rem(tile, 2)
    return x, z, y, lax.rem(orient, 2)


def device(x, z, y, core):
    return (x * 16 + z * 2 + lax.rem(y, 2), lax.div(y, 2) * 2 + core)


def remote(src, dst, send, recv, target):
    return pltpu.make_async_remote_copy(
        src_ref=src, dst_ref=dst, send_sem=send, recv_sem=recv, device_id=target, device_id_type=MESH
    )


def dot(a, b):
    return jnp.dot(a, b, preferred_element_type=F32)


def rotate(block, quarter):
    turns = jnp.full((256, 256), quarter, jnp.int32)
    row = lax.broadcasted_iota(jnp.int32, (256, 256), 0)
    col = lax.broadcasted_iota(jnp.int32, (256, 256), 1)
    same = (row == col).astype(F32)
    swapped = (row + col == 255).astype(F32)
    flip_rows = jnp.where((turns == 1) | (turns == 2), swapped, same).astype(BF)
    flip_cols = jnp.where((turns == 2) | (turns == 3), swapped, same).astype(BF)
    wide = block.astype(F32)
    turned = jnp.where((turns == 1) | (turns == 3), wide.T, wide).astype(BF)
    return dot(dot(flip_rows, turned).astype(BF), flip_cols).astype(BF)


def tile_spectrum(mic, fwd, fwd_t, work, spec):
    quarters = [mic[0, 128 * q : 128 * q + 128, :].astype(F32) for q in range(4)]
    a, b = quarters[0] + quarters[2], quarters[1] + quarters[3]
    c, d = quarters[0] - quarters[2], quarters[1] - quarters[3]
    outs = [
        dot(fwd[0, :, :128], (a + b).astype(BF)),
        dot(fwd[1], jnp.concatenate([c, -d], axis=0).astype(BF)),
        dot(fwd[2, :, :128], (a - b).astype(BF)),
        dot(fwd[3], jnp.concatenate([c, d], axis=0).astype(BF)),
    ]
    for r1 in range(4):
        re = [outs[r1][:128, 128 * p : 128 * p + 128] for p in range(4)]
        im = [outs[r1][128:, 128 * p : 128 * p + 128] for p in range(4)]
        rows = pl.ds(128 * r1, 128)
        rs, rd, im_s, im_d = re[0] + re[2], re[0] - re[2], im[0] + im[2], im[0] - im[2]
        ro, rp, io, ip = re[1] + re[3], re[1] - re[3], im[1] + im[3], im[1] - im[3]
        pairs = [(rs + ro, im_s + io), (rd + ip, im_d - rp), (rs - ro, im_s - io), (rd - ip, im_d + rp)]
        for r2, (p_re, p_im) in enumerate(pairs):
            work[r2, rows, :128] = p_re.astype(BF)
            work[r2, rows, 128:] = p_im.astype(BF)
    for r2 in range(4):
        spec[r2] = dot(work[r2], fwd_t[r2]).astype(BF)


def inverse_rows(fwd_t, quarter, left):
    for r in range(4):
        turn = lax.rem(quarter * r, 4)
        turn = jnp.full((128, 128), turn, jnp.int32)
        c = fwd_t[r, :128, :128].astype(F32)
        s = fwd_t[r, 128:, :128].astype(F32)
        new_c = jnp.where(turn == 0, c, jnp.where(turn == 1, -s, jnp.where(turn == 2, -c, s))).astype(BF)
        new_s = jnp.where(turn == 0, s, jnp.where(turn == 1, c, jnp.where(turn == 2, -s, -c)))
        left[:128, 256 * r : 256 * r + 128] = new_c
        left[128:, 256 * r + 128 : 256 * r + 256] = new_c
        left[:128, 256 * r + 128 : 256 * r + 256] = (-new_s).astype(BF)
        left[128:, 256 * r : 256 * r + 128] = new_s.astype(BF)


def pair_scores(block, fwd, fwd_t, spec, left, work, prod, best, total, first):
    a0, a1 = [jnp.concatenate([block(q, 0, 0), block(q, 1, 0)], axis=1).astype(F32) for q in range(2)]
    b0, b1 = [jnp.concatenate([block(q, 0, 1), block(q, 1, 1)], axis=1).astype(F32) for q in range(2)]
    stacked = [(a0 + a1, b0 + b1), (a0 + b1, b0 - a1), (a0 - a1, b0 - b1), (a0 - b1, b0 + a1)]
    for r1 in range(4):
        out = dot(fwd[r1], jnp.concatenate(stacked[r1], axis=0).astype(BF))
        re0, re1, im0, im1 = out[:128, :128], out[:128, 128:], out[128:, :128], out[128:, 128:]
        rows = pl.ds(128 * r1, 128)
        pairs = [(re0 + re1, im0 + im1), (re0 + im1, im0 - re1), (re0 - re1, im0 - im1), (re0 - im1, im0 + re1)]
        for r2, (p_re, p_im) in enumerate(pairs):
            work[r2, rows, :128] = p_re.astype(BF)
            work[r2, rows, 128:] = p_im.astype(BF)
    for r2 in range(4):
        found = dot(work[r2], fwd_t[r2])
        t_re, t_im = found[:, :128].astype(BF).astype(F32), found[:, 128:].astype(BF).astype(F32)
        x_re, x_im = spec[r2, :, :128].astype(F32), spec[r2, :, 128:].astype(F32)
        p_re = (x_re * t_re + x_im * t_im).astype(BF)
        p_im = (x_im * t_re - x_re * t_im).astype(BF)
        lanes = pl.ds(128 * r2, 128)
        for r1 in range(4):
            prod[pl.ds(256 * r1, 128), lanes] = p_re[128 * r1 : 128 * r1 + 128]
            prod[pl.ds(256 * r1 + 128, 128), lanes] = p_im[128 * r1 : 128 * r1 + 128]
    mid = dot(left[...], prod[...]).astype(BF)
    u = []
    for r2 in range(4):
        lanes = slice(128 * r2, 128 * r2 + 128)
        u.append(dot(jnp.concatenate([mid[:128, lanes], mid[128:, lanes]], axis=1), fwd[r2]))
    re = [v[:, :128] for v in u]
    im = [v[:, 128:] for v in u]
    rs, rd, im_s, im_d = re[0] + re[2], re[0] - re[2], im[0] + im[2], im[0] - im[2]
    ro, rp, io, ip = re[1] + re[3], re[1] - re[3], im[1] + im[3], im[1] - im[3]
    one = [rs + ro, rd - ip, rs - ro, rd + ip]
    two = [-(im_s + io), -(im_d + rp), io - im_s, rp - im_d]
    for q in range(4):
        lanes = pl.ds(128 * q, 128)
        top, both = jnp.maximum(one[q], two[q]), one[q] + two[q]
        if first:
            best[:, lanes] = top
            total[:, lanes] = both
        else:
            best[:, lanes] = jnp.maximum(best[:, lanes], top)
            total[:, lanes] = total[:, lanes] + both


def kernel(
    quarter_in, plan_in, mic_in, tmpl_in, fwd_in, fwd_t_in, out,
    quarter, plan, mic, tmpl, fwd, fwd_t, load, turned, got, line, tx, tz, spec, work, prod, left, best, total, give, take,
    a_send, a_recv, y_send, y_recv, sx_send, sx_recv, sz_send, sz_recv, lz_send, lz_recv, bx_send, bx_recv, bz_send, bz_recv, c_send, c_recv,
):
    x, z, y, core = coords()
    early = z < 4
    late = z >= 4
    x_ways = [lax.rem(x + d, 4) for d in (2, 1, 3)]
    x_peers = [device(px, z, y, core) for px in x_ways]
    y_peers = [device(x, z, lax.rem(y + d, 8), core) for d in (4, 3, 5, 2, 6, 1, 7)]
    part = jnp.where(early, z, 7 - z)
    others = [k + (part <= k).astype(jnp.int32) for k in range(3)]
    z_peers = [device(x, jnp.where(early, k, 7 - k), y, core) for k in others]
    partner = device(x, 7 - z, y, core)
    other = device(x, z, y, 1 - core)
    columns = x_ways + [x]

    barrier = pltpu.get_barrier_semaphore()

    def greet(target):
        pl.semaphore_signal(barrier, inc=1, device_id=target, device_id_type=MESH)

    @pl.when(early)
    def _():
        for px in columns:
            for pz in (7, 6, 5, 4, 3, 2, 1, 0):

                @pl.when((px != x) | (z != pz))
                def _():
                    greet(device(px, pz, y, core))

        for target in y_peers:
            greet(target)

    greet(other)
    loads = [
        pltpu.make_async_copy(src, dst, load.at[i])
        for i, (src, dst) in enumerate(
            [(quarter_in, quarter), (tmpl_in, tmpl), (fwd_in, fwd), (mic_in, mic), (fwd_t_in, fwd_t), (plan_in, plan)]
        )
    ]
    for copy in loads:
        copy.start()
    loads[0].wait()
    loads[1].wait()

    block = rotate(tmpl[0, 0], quarter[0, 0])
    for q in range(2):
        for h in range(2):
            chunks = block[128 * q : 128 * q + 128, 128 * h : 128 * h + 128].reshape(4, 2, 16, 128)
            turned[pl.ds(8 * q + 4 * h, 4)] = chunks

    @pl.when(early)
    def _():
        pl.semaphore_wait(barrier, 23)

    @pl.when(late)
    def _():
        pl.semaphore_wait(barrier, 17)

    mine = x * 8 + z

    def scatter(k, pz):
        px = columns[k]
        return remote(
            turned.at[px * 4 + pz], got.at[mine], a_send.at[4 * k + pz], a_recv.at[mine], device(px, pz, y, core)
        )

    for k in range(4):
        for pz in (3, 0, 2, 1):

            @pl.when((z != pz) if k == 3 else (z >= 0))
            def _():
                scatter(k, pz).start()

    for copy in loads[2:]:
        copy.wait()
    tile_spectrum(mic, fwd, fwd_t, work, spec)
    inverse_rows(fwd_t, lax.div(y, 2), left)

    mine_z = pl.ds(2 * part, 2)

    def z_first(p, i):
        ref = tx.at[x, p, mine_z]
        return remote(ref, ref, sz_send.at[p, i], sz_recv.at[p, part], z_peers[i])

    def z_first_from(p, k):
        ref = tx.at[x, p, pl.ds(2 * k, 2)]
        return remote(ref, ref, sz_send.at[p, 0], sz_recv.at[p, k], other)

    def x_first(i):
        ref = tz.at[mine_z, x]
        return remote(ref, ref, sx_send.at[i], sx_recv.at[i], x_peers[i])

    def z_last(i):
        return remote(tz.at[mine_z], tz.at[mine_z], bz_send.at[i], bz_recv.at[part], z_peers[i])

    def z_last_from(k):
        ref = tz.at[pl.ds(2 * k, 2)]
        return remote(ref, ref, bz_send.at[0], bz_recv.at[k], other)

    def across(p):
        ref = tz.at[mine_z, x] if p == 3 else tx.at[x, p, mine_z]
        return remote(ref, ref, lz_send.at[p], lz_recv.at[p], partner)

    def x_last(p, i):
        return remote(tx.at[x, p], tx.at[x, p], bx_send.at[p, i], bx_recv.at[p, i], x_peers[i])

    def to_y(i):
        return remote(line.at[y], line.at[y], y_send.at[i], y_recv.at[y], y_peers[i])

    @pl.when(early)
    def _():
        got[mine] = turned[x * 4 + z]
        for k in range(4):
            for pz in range(8):
                source = columns[k] * 8 + pz

                @pl.when((z != pz) if k == 3 else (z >= 0))
                def _():
                    remote(turned.at[0], got.at[source], a_send.at[0], a_recv.at[source], other).wait_recv()

        owners = [plan[s] for s in range(2)]
        for s in range(2):
            line[y, s] = got[lax.div(owners[s], 2)]
        for i in range(7):
            to_y(i).start()
        odd = [jnp.full((2, 16, 128), lax.rem(owners[s], 2), jnp.int32) for s in range(2)]

        def arrived(pair):
            for low in range(2):
                source = 2 * pair + low

                @pl.when(source != y)
                def _():
                    remote(line.at[source], line.at[source], y_send.at[0], y_recv.at[source], other).wait_recv()

            return [jnp.where(odd[s] == 0, line[2 * pair, s], line[2 * pair + 1, s]) for s in range(2)]

        own = lax.div(y, 2)
        for s, tiles in enumerate(arrived(own)):
            for b in range(2):
                tz[2 * z + b, x, s] = tiles[b]
        for i in range(3):
            x_first(i).start()
        across(3).start()
        for p, pairs in enumerate(((1, 0, 1, 0), (3, 3, 3, 1), (2, 2, 0, 2))):
            chosen = jnp.where(own < 2, jnp.where(own == 0, pairs[0], pairs[1]), jnp.where(own == 2, pairs[2], pairs[3]))
            for s, tiles in enumerate(arrived(chosen)):
                for b in range(2):
                    tx[x, p, 2 * z + b, s] = tiles[b]
            for i in range(3):
                z_first(p, i).start()
            across(p).start()

    @pl.when(late)
    def _():
        across(3).wait_recv()
        for i in range(3):
            x_first(i).start()
        for p in range(3):
            across(p).wait_recv()
            for i in range(3):
                z_first(p, i).start()

    for i in range(3):
        x_first(i).wait_recv()
    for i in range(3):
        z_last(i).start()
    for p in range(3):
        for k in others:
            z_first_from(p, k).wait_recv()
        for i in range(3):
            x_last(p, i).start()

    def from_x(p):
        return lambda q, h, s: tx[2 * q + h, p, :, s].reshape(128, 128)

    def from_z(q, h, s):
        return tz[:, 2 * q + h, s].reshape(128, 128)

    for i in range(3):
        x_last(0, i).wait_recv()
    pair_scores(from_x(0), fwd, fwd_t, spec, left, work, prod, best, total, True)

    for k in others:
        z_last_from(k).wait_recv()
    pair_scores(from_z, fwd, fwd_t, spec, left, work, prod, best, total, False)
    for p in range(1, 3):
        for i in range(3):
            x_last(p, i).wait_recv()
        pair_scores(from_x(p), fwd, fwd_t, spec, left, work, prod, best, total, False)

    theirs, ours = pl.ds((1 - core) * 64, 64), pl.ds(core * 64, 64)
    give[0] = best[theirs, :].astype(BF)
    give[1] = total[theirs, :].astype(BF)
    swap = remote(give, take, c_send, c_recv, other)
    swap.start()
    swap.wait_recv()
    out[0] = jnp.maximum(best[ours, :], take[0].astype(F32))
    out[1] = total[ours, :] + take[1].astype(F32)
    swap.wait_send()
    for k in range(4):
        for pz in range(4):

            @pl.when((z != pz) if k == 3 else (z >= 0))
            def _():
                scatter(k, pz).wait_send()

    for i in range(3):
        x_first(i).wait_send()
        z_last(i).wait_send()
        for p in range(3):
            z_first(p, i).wait_send()
            x_last(p, i).wait_send()

    @pl.when(early)
    def _():
        for i in range(7):
            to_y(i).wait_send()
        for p in range(4):
            across(p).wait_send()


def per_device(micrographs, templates, quarter_turns, plan):
    fwd, fwd_t = radix_tables()
    dma = pltpu.SemaphoreType.DMA
    raw = pl.pallas_call(
        kernel,
        out_shape=jax.ShapeDtypeStruct((2, 64, SIDE), F32),
        in_specs=[pl.BlockSpec(memory_space=pltpu.HBM)] * 6,
        out_specs=pl.BlockSpec(memory_space=pltpu.VMEM),
        scratch_shapes=[
            pltpu.SMEM((1, 1), jnp.int32),
            pltpu.SMEM((64,), jnp.int32),
            pltpu.VMEM((1, SIDE, SIDE), BF),
            pltpu.VMEM((1, 1, 256, 256), BF),
            pltpu.VMEM((4, 256, 256), BF),
            pltpu.VMEM((4, 256, 256), BF),
            dma((6,)),
            pltpu.VMEM((16, 2, 16, 128), BF),
            pltpu.VMEM((32, 2, 16, 128), BF),
            pltpu.VMEM((8, 2, 2, 16, 128), BF),
            pltpu.VMEM((4, 3, 8, 2, 16, 128), BF),
            pltpu.VMEM((8, 4, 2, 16, 128), BF),
            pltpu.VMEM((4, 512, 256), BF),
            pltpu.VMEM((4, 512, 256), BF),
            pltpu.VMEM((1024, 512), BF),
            pltpu.VMEM((256, 1024), BF),
            pltpu.VMEM((128, 512), F32),
            pltpu.VMEM((128, 512), F32),
            pltpu.VMEM((2, 64, 512), BF),
            pltpu.VMEM((2, 64, 512), BF),
            dma((16,)), dma((32,)), dma((7,)), dma((8,)), dma((3,)), dma((3,)), dma((3, 3)), dma((3, 4)), dma((4,)), dma((4,)),
            dma((3, 3)), dma((3, 3)), dma((3,)), dma((4,)), dma(()), dma(()),
        ],
        compiler_params=pltpu.CompilerParams(collective_id=0, has_side_effects=True, vmem_limit_bytes=107 << 19),
        name="match",
    )(quarter_turns, plan, micrographs, templates, jnp.asarray(fwd), jnp.asarray(fwd_t))
    scale = 1.0 / (SIDE * SIDE)
    return raw[0:1] * scale, raw[1:2] * (scale / SEARCHED)


def solution(mesh):
    in_specs = (P("tile", None, None), P("tile", "orient", None, None), P("tile", "orient"), P())
    out_specs = (P("tile", "orient", None), P("tile", "orient", None))
    return jax.shard_map(per_device, mesh=mesh, in_specs=in_specs, out_specs=out_specs, check_vma=False)
```

```python
import functools

import jax
import jax.numpy as jnp
import numpy as np
from jax import lax
from jax.experimental import pallas as pl
from jax.experimental.pallas import tpu as pltpu
from jax.sharding import PartitionSpec as P

MESH = pl.DeviceIdType.MESH
BF = jnp.bfloat16
F32 = jnp.float32
SIDE = 512
SEARCHED = 16


def radix_tables():
    j = np.arange(128)
    forward = []
    for r in range(4):
        phase = (np.outer(4 * j + r, j) % SIDE).astype(np.float32)
        angle = np.float32(2.0 * np.pi / SIDE) * phase
        c, s = np.cos(angle), np.sin(angle)
        forward.append(np.block([[c, s], [-s, c]]))
    forward = np.stack(forward).astype(np.float32)
    return forward.astype(jnp.bfloat16), forward.transpose(0, 2, 1).astype(jnp.bfloat16)


def coords():
    tile = lax.axis_index("tile")
    orient = lax.axis_index("orient")
    x, z = lax.div(tile, 16), lax.rem(lax.div(tile, 2), 8)
    y = lax.div(orient, 2) * 2 + lax.rem(tile, 2)
    return x, z, y, lax.rem(orient, 2)


def device(x, z, y, core):
    return (x * 16 + z * 2 + lax.rem(y, 2), lax.div(y, 2) * 2 + core)


def remote(src, dst, send, recv, target):
    return pltpu.make_async_remote_copy(
        src_ref=src, dst_ref=dst, send_sem=send, recv_sem=recv, device_id=target, device_id_type=MESH
    )


def dot(a, b):
    return jnp.dot(a, b, preferred_element_type=F32)


def rotate(block, quarter):
    turns = jnp.full((256, 256), quarter, jnp.int32)
    row = lax.broadcasted_iota(jnp.int32, (256, 256), 0)
    col = lax.broadcasted_iota(jnp.int32, (256, 256), 1)
    same = (row == col).astype(F32)
    swapped = (row + col == 255).astype(F32)
    flip_rows = jnp.where((turns == 1) | (turns == 2), swapped, same).astype(BF)
    flip_cols = jnp.where((turns == 2) | (turns == 3), swapped, same).astype(BF)
    wide = block.astype(F32)
    turned = jnp.where((turns == 1) | (turns == 3), wide.T, wide).astype(BF)
    return dot(dot(flip_rows, turned).astype(BF), flip_cols).astype(BF)


def tile_spectrum(mic, fwd, fwd_t, work, spec):
    quarters = [mic[0, 128 * q : 128 * q + 128, :].astype(F32) for q in range(4)]
    a, b = quarters[0] + quarters[2], quarters[1] + quarters[3]
    c, d = quarters[0] - quarters[2], quarters[1] - quarters[3]
    outs = [
        dot(fwd[0, :, :128], (a + b).astype(BF)),
        dot(fwd[1], jnp.concatenate([c, -d], axis=0).astype(BF)),
        dot(fwd[2, :, :128], (a - b).astype(BF)),
        dot(fwd[3], jnp.concatenate([c, d], axis=0).astype(BF)),
    ]
    for r1 in range(4):
        re = [outs[r1][:128, 128 * p : 128 * p + 128] for p in range(4)]
        im = [outs[r1][128:, 128 * p : 128 * p + 128] for p in range(4)]
        rows = pl.ds(128 * r1, 128)
        rs, rd, im_s, im_d = re[0] + re[2], re[0] - re[2], im[0] + im[2], im[0] - im[2]
        ro, rp, io, ip = re[1] + re[3], re[1] - re[3], im[1] + im[3], im[1] - im[3]
        pairs = [(rs + ro, im_s + io), (rd + ip, im_d - rp), (rs - ro, im_s - io), (rd - ip, im_d + rp)]
        for r2, (p_re, p_im) in enumerate(pairs):
            work[r2, rows, :128] = p_re.astype(BF)
            work[r2, rows, 128:] = p_im.astype(BF)
    for r2 in range(4):
        spec[r2] = dot(work[r2], fwd_t[r2]).astype(BF)


def inverse_rows(fwd_t, quarter, left):
    for r in range(4):
        turn = lax.rem(quarter * r, 4)
        turn = jnp.full((128, 128), turn, jnp.int32)
        c = fwd_t[r, :128, :128].astype(F32)
        s = fwd_t[r, 128:, :128].astype(F32)
        new_c = jnp.where(turn == 0, c, jnp.where(turn == 1, -s, jnp.where(turn == 2, -c, s))).astype(BF)
        new_s = jnp.where(turn == 0, s, jnp.where(turn == 1, c, jnp.where(turn == 2, -s, -c)))
        left[:128, 256 * r : 256 * r + 128] = new_c
        left[128:, 256 * r + 128 : 256 * r + 256] = new_c
        left[:128, 256 * r + 128 : 256 * r + 256] = (-new_s).astype(BF)
        left[128:, 256 * r : 256 * r + 128] = new_s.astype(BF)


def pair_scores(block, fwd, fwd_t, spec, left, work, prod, best, total, first):
    a0, a1 = [jnp.concatenate([block(q, 0, 0), block(q, 1, 0)], axis=1) for q in range(2)]
    b0, b1 = [jnp.concatenate([block(q, 0, 1), block(q, 1, 1)], axis=1) for q in range(2)]
    stacked = [(a0 + a1, b0 + b1), (a0 + b1, b0 - a1), (a0 - a1, b0 - b1), (a0 - b1, b0 + a1)]
    for r1 in range(4):
        out = dot(fwd[r1], jnp.concatenate(stacked[r1], axis=0))
        re0, re1, im0, im1 = out[:128, :128], out[:128, 128:], out[128:, :128], out[128:, 128:]
        rows = pl.ds(128 * r1, 128)
        pairs = [(re0 + re1, im0 + im1), (re0 + im1, im0 - re1), (re0 - re1, im0 - im1), (re0 - im1, im0 + re1)]
        for r2, (p_re, p_im) in enumerate(pairs):
            work[r2, rows, :128] = p_re.astype(BF)
            work[r2, rows, 128:] = p_im.astype(BF)
    for r2 in range(4):
        found = dot(work[r2], fwd_t[r2])
        t_re, t_im = found[:, :128].astype(BF), found[:, 128:].astype(BF)
        x_re, x_im = spec[r2, :, :128], spec[r2, :, 128:]
        p_re = x_re * t_re + x_im * t_im
        p_im = x_im * t_re - x_re * t_im
        lanes = pl.ds(128 * r2, 128)
        for r1 in range(4):
            prod[pl.ds(256 * r1, 128), lanes] = p_re[128 * r1 : 128 * r1 + 128]
            prod[pl.ds(256 * r1 + 128, 128), lanes] = p_im[128 * r1 : 128 * r1 + 128]
    mid = dot(left[...], prod[...]).astype(BF)
    u = []
    for r2 in range(4):
        lanes = slice(128 * r2, 128 * r2 + 128)
        u.append(dot(jnp.concatenate([mid[:128, lanes], mid[128:, lanes]], axis=1), fwd[r2]))
    re = [v[:, :128] for v in u]
    im = [v[:, 128:] for v in u]
    rs, rd, im_s, im_d = re[0] + re[2], re[0] - re[2], im[0] + im[2], im[0] - im[2]
    ro, rp, io, ip = re[1] + re[3], re[1] - re[3], im[1] + im[3], im[1] - im[3]
    one = [rs + ro, rd - ip, rs - ro, rd + ip]
    two = [-(im_s + io), -(im_d + rp), io - im_s, rp - im_d]
    for q in range(4):
        lanes = pl.ds(128 * q, 128)
        top, both = jnp.maximum(one[q], two[q]), one[q] + two[q]
        if first:
            best[:, lanes] = top
            total[:, lanes] = both
        else:
            best[:, lanes] = jnp.maximum(best[:, lanes], top)
            total[:, lanes] = total[:, lanes] + both


def kernel(
    quarter_in, plan_in, mic_in, tmpl_in, fwd_in, fwd_t_in, out,
    quarter, plan, mic, tmpl, fwd, fwd_t, load, turned, got, line, tx, tz, spec, work, prod, left, best, total, give, take,
    a_send, a_recv, y_send, y_recv, sx_send, sx_recv, sz_send, sz_recv, lz_send, lz_recv, bx_send, bx_recv, bz_send, bz_recv, c_send, c_recv,
):
    x, z, y, core = coords()
    early = z < 4
    late = z >= 4
    x_ways = [lax.rem(x + d, 4) for d in (2, 1, 3)]
    x_peers = [device(px, z, y, core) for px in x_ways]
    y_peers = [device(x, z, lax.rem(y + d, 8), core) for d in (4, 3, 5, 2, 6, 1, 7)]
    part = jnp.where(early, z, 7 - z)
    others = [k + (part <= k).astype(jnp.int32) for k in range(3)]
    z_peers = [device(x, jnp.where(early, k, 7 - k), y, core) for k in others]
    partner = device(x, 7 - z, y, core)
    other = device(x, z, y, 1 - core)
    columns = x_ways + [x]

    barrier = pltpu.get_barrier_semaphore()

    def greet(target):
        pl.semaphore_signal(barrier, inc=1, device_id=target, device_id_type=MESH)

    @pl.when(early)
    def _():
        for px in columns:
            for pz in (7, 6, 5, 4, 3, 2, 1, 0):

                @pl.when((px != x) | (z != pz))
                def _():
                    greet(device(px, pz, y, core))

        for target in y_peers:
            greet(target)

    greet(other)
    loads = [
        pltpu.make_async_copy(src, dst, load.at[i])
        for i, (src, dst) in enumerate(
            [(quarter_in, quarter), (tmpl_in, tmpl), (fwd_in, fwd), (mic_in, mic), (fwd_t_in, fwd_t), (plan_in, plan)]
        )
    ]
    for copy in loads:
        copy.start()
    loads[0].wait()
    loads[1].wait()

    block = rotate(tmpl[0, 0], quarter[0, 0])
    for q in range(2):
        for h in range(2):
            chunks = block[128 * q : 128 * q + 128, 128 * h : 128 * h + 128].reshape(4, 2, 16, 128)
            turned[pl.ds(8 * q + 4 * h, 4)] = chunks

    @pl.when(early)
    def _():
        pl.semaphore_wait(barrier, 23)

    @pl.when(late)
    def _():
        pl.semaphore_wait(barrier, 17)

    mine = x * 8 + z

    def scatter(k, pz):
        px = columns[k]
        return remote(
            turned.at[px * 4 + pz], got.at[mine], a_send.at[4 * k + pz], a_recv.at[mine], device(px, pz, y, core)
        )

    for k in range(4):
        for pz in (3, 0, 2, 1):

            @pl.when((z != pz) if k == 3 else (z >= 0))
            def _():
                scatter(k, pz).start()

    for copy in loads[2:]:
        copy.wait()
    tile_spectrum(mic, fwd, fwd_t, work, spec)
    inverse_rows(fwd_t, lax.div(y, 2), left)

    mine_z = pl.ds(2 * part, 2)

    def z_first(p, i):
        ref = tx.at[x, p, mine_z]
        return remote(ref, ref, sz_send.at[p, i], sz_recv.at[p, part], z_peers[i])

    def z_first_from(p, k):
        ref = tx.at[x, p, pl.ds(2 * k, 2)]
        return remote(ref, ref, sz_send.at[p, 0], sz_recv.at[p, k], other)

    def x_first(i):
        ref = tz.at[mine_z, x]
        return remote(ref, ref, sx_send.at[i], sx_recv.at[i], x_peers[i])

    def z_last(i):
        return remote(tz.at[mine_z], tz.at[mine_z], bz_send.at[i], bz_recv.at[part], z_peers[i])

    def z_last_from(k):
        ref = tz.at[pl.ds(2 * k, 2)]
        return remote(ref, ref, bz_send.at[0], bz_recv.at[k], other)

    def across(p):
        ref = tz.at[mine_z, x] if p == 3 else tx.at[x, p, mine_z]
        return remote(ref, ref, lz_send.at[p], lz_recv.at[p], partner)

    def x_last(p, i):
        return remote(tx.at[x, p], tx.at[x, p], bx_send.at[p, i], bx_recv.at[p, i], x_peers[i])

    def to_y(i):
        return remote(line.at[y], line.at[y], y_send.at[i], y_recv.at[y], y_peers[i])

    @pl.when(early)
    def _():
        got[mine] = turned[x * 4 + z]
        for k in range(4):
            for pz in range(8):
                source = columns[k] * 8 + pz

                @pl.when((z != pz) if k == 3 else (z >= 0))
                def _():
                    remote(turned.at[0], got.at[source], a_send.at[0], a_recv.at[source], other).wait_recv()

        owners = [plan[s] for s in range(2)]
        for s in range(2):
            line[y, s] = got[lax.div(owners[s], 2)]
        for i in range(7):
            to_y(i).start()
        odd = [jnp.full((2, 16, 128), lax.rem(owners[s], 2), jnp.int32) for s in range(2)]

        def arrived(pair):
            for low in range(2):
                source = 2 * pair + low

                @pl.when(source != y)
                def _():
                    remote(line.at[source], line.at[source], y_send.at[0], y_recv.at[source], other).wait_recv()

            return [jnp.where(odd[s] == 0, line[2 * pair, s], line[2 * pair + 1, s]) for s in range(2)]

        own = lax.div(y, 2)
        for s, tiles in enumerate(arrived(own)):
            for b in range(2):
                tz[2 * z + b, x, s] = tiles[b]
        for i in range(3):
            x_first(i).start()
        across(3).start()
        for p, pairs in enumerate(((1, 0, 1, 0), (3, 3, 3, 1), (2, 2, 0, 2))):
            chosen = jnp.where(own < 2, jnp.where(own == 0, pairs[0], pairs[1]), jnp.where(own == 2, pairs[2], pairs[3]))
            for s, tiles in enumerate(arrived(chosen)):
                for b in range(2):
                    tx[x, p, 2 * z + b, s] = tiles[b]
            for i in range(3):
                z_first(p, i).start()
            across(p).start()

    @pl.when(late)
    def _():
        across(3).wait_recv()
        for i in range(3):
            x_first(i).start()
        for p in range(3):
            across(p).wait_recv()
            for i in range(3):
                z_first(p, i).start()

    for i in range(3):
        x_first(i).wait_recv()
    for i in range(3):
        z_last(i).start()
    for p in range(3):
        for k in others:
            z_first_from(p, k).wait_recv()
        for i in range(3):
            x_last(p, i).start()

    def from_x(p):
        return lambda q, h, s: tx[2 * q + h, p, :, s].reshape(128, 128)

    def from_z(q, h, s):
        return tz[:, 2 * q + h, s].reshape(128, 128)

    for i in range(3):
        x_last(0, i).wait_recv()
    pair_scores(from_x(0), fwd, fwd_t, spec, left, work, prod, best, total, True)

    for k in others:
        z_last_from(k).wait_recv()
    pair_scores(from_z, fwd, fwd_t, spec, left, work, prod, best, total, False)
    for p in range(1, 3):
        for i in range(3):
            x_last(p, i).wait_recv()
        pair_scores(from_x(p), fwd, fwd_t, spec, left, work, prod, best, total, False)

    theirs, ours = pl.ds((1 - core) * 64, 64), pl.ds(core * 64, 64)
    give[0] = best[theirs, :].astype(BF)
    give[1] = total[theirs, :].astype(BF)
    swap = remote(give, take, c_send, c_recv, other)
    swap.start()
    swap.wait_recv()
    out[0] = jnp.maximum(best[ours, :], take[0].astype(F32))
    out[1] = total[ours, :] + take[1].astype(F32)
    swap.wait_send()
    for k in range(4):
        for pz in range(4):

            @pl.when((z != pz) if k == 3 else (z >= 0))
            def _():
                scatter(k, pz).wait_send()

    for i in range(3):
        x_first(i).wait_send()
        z_last(i).wait_send()
        for p in range(3):
            z_first(p, i).wait_send()
            x_last(p, i).wait_send()

    @pl.when(early)
    def _():
        for i in range(7):
            to_y(i).wait_send()
        for p in range(4):
            across(p).wait_send()


def per_device(micrographs, templates, quarter_turns, plan):
    fwd, fwd_t = radix_tables()
    dma = pltpu.SemaphoreType.DMA
    operands = (quarter_turns, plan, micrographs, templates, jnp.asarray(fwd), jnp.asarray(fwd_t))
    raw = pl.pallas_call(
        kernel,
        out_shape=jax.ShapeDtypeStruct((2, 64, SIDE), F32),
        in_specs=[pl.BlockSpec(memory_space=pltpu.HBM)] * 6,
        out_specs=pl.BlockSpec(memory_space=pltpu.VMEM),
        scratch_shapes=[
            pltpu.SMEM((1, 1), jnp.int32),
            pltpu.SMEM((64,), jnp.int32),
            pltpu.VMEM((1, SIDE, SIDE), BF),
            pltpu.VMEM((1, 1, 256, 256), BF),
            pltpu.VMEM((4, 256, 256), BF),
            pltpu.VMEM((4, 256, 256), BF),
            dma((6,)),
            pltpu.VMEM((16, 2, 16, 128), BF),
            pltpu.VMEM((32, 2, 16, 128), BF),
            pltpu.VMEM((8, 2, 2, 16, 128), BF),
            pltpu.VMEM((4, 3, 8, 2, 16, 128), BF),
            pltpu.VMEM((8, 4, 2, 16, 128), BF),
            pltpu.VMEM((4, 512, 256), BF),
            pltpu.VMEM((4, 512, 256), BF),
            pltpu.VMEM((1024, 512), BF),
            pltpu.VMEM((256, 1024), BF),
            pltpu.VMEM((128, 512), F32),
            pltpu.VMEM((128, 512), F32),
            pltpu.VMEM((2, 64, 512), BF),
            pltpu.VMEM((2, 64, 512), BF),
            dma((16,)), dma((32,)), dma((7,)), dma((8,)), dma((3,)), dma((3,)), dma((3, 3)), dma((3, 4)), dma((4,)), dma((4,)),
            dma((3, 3)), dma((3, 3)), dma((3,)), dma((4,)), dma(()), dma(()),
        ],
        compiler_params=pltpu.CompilerParams(collective_id=0, has_side_effects=True, vmem_limit_bytes=40 << 20),
        name="match",
    )(operands[0], *[pltpu.with_memory_space_constraint(a, pltpu.HBM) for a in operands[1:]])
    scale = 1.0 / (SIDE * SIDE)
    return raw[0:1] * scale, raw[1:2] * (scale / SEARCHED)


def solution(mesh):
    in_specs = (P("tile", None, None), P("tile", "orient", None, None), P("tile", "orient"), P())
    out_specs = (P("tile", "orient", None), P("tile", "orient", None))
    return jax.shard_map(per_device, mesh=mesh, in_specs=in_specs, out_specs=out_specs, check_vma=False)
```

```python
import functools

import jax
import jax.numpy as jnp
import numpy as np
from jax import lax
from jax.experimental import pallas as pl
from jax.experimental.pallas import tpu as pltpu
from jax.sharding import PartitionSpec as P

MESH = pl.DeviceIdType.MESH
BF = jnp.bfloat16
F32 = jnp.float32
SIDE = 512
SEARCHED = 16


def radix_tables():
    j = np.arange(128)
    forward = []
    for r in range(4):
        phase = (np.outer(4 * j + r, j) % SIDE).astype(np.float32)
        angle = np.float32(2.0 * np.pi / SIDE) * phase
        c, s = np.cos(angle), np.sin(angle)
        forward.append(np.block([[c, s], [-s, c]]))
    forward = np.stack(forward).astype(np.float32)
    return forward.astype(jnp.bfloat16), forward.transpose(0, 2, 1).astype(jnp.bfloat16)


def coords():
    tile = lax.axis_index("tile")
    orient = lax.axis_index("orient")
    x, z = lax.div(tile, 16), lax.rem(lax.div(tile, 2), 8)
    y = lax.div(orient, 2) * 2 + lax.rem(tile, 2)
    return x, z, y, lax.rem(orient, 2)


def device(x, z, y, core):
    return (x * 16 + z * 2 + lax.rem(y, 2), lax.div(y, 2) * 2 + core)


def remote(src, dst, send, recv, target):
    return pltpu.make_async_remote_copy(
        src_ref=src, dst_ref=dst, send_sem=send, recv_sem=recv, device_id=target, device_id_type=MESH
    )


def dot(a, b):
    return jnp.dot(a, b, preferred_element_type=F32)


def rotate(block, quarter):
    turns = jnp.full((256, 256), quarter, jnp.int32)
    row = lax.broadcasted_iota(jnp.int32, (256, 256), 0)
    col = lax.broadcasted_iota(jnp.int32, (256, 256), 1)
    same = (row == col).astype(F32)
    swapped = (row + col == 255).astype(F32)
    flip_rows = jnp.where((turns == 1) | (turns == 2), swapped, same).astype(BF)
    flip_cols = jnp.where((turns == 2) | (turns == 3), swapped, same).astype(BF)
    wide = block.astype(F32)
    turned = jnp.where((turns == 1) | (turns == 3), wide.T, wide).astype(BF)
    return dot(dot(flip_rows, turned).astype(BF), flip_cols).astype(BF)


def tile_spectrum(mic, fwd, fwd_t, work, spec):
    quarters = [mic[0, 128 * q : 128 * q + 128, :].astype(F32) for q in range(4)]
    a, b = quarters[0] + quarters[2], quarters[1] + quarters[3]
    c, d = quarters[0] - quarters[2], quarters[1] - quarters[3]
    outs = [
        dot(fwd[0, :, :128], (a + b).astype(BF)),
        dot(fwd[1], jnp.concatenate([c, -d], axis=0).astype(BF)),
        dot(fwd[2, :, :128], (a - b).astype(BF)),
        dot(fwd[3], jnp.concatenate([c, d], axis=0).astype(BF)),
    ]
    for r1 in range(4):
        re = [outs[r1][:128, 128 * p : 128 * p + 128] for p in range(4)]
        im = [outs[r1][128:, 128 * p : 128 * p + 128] for p in range(4)]
        rows = pl.ds(128 * r1, 128)
        rs, rd, im_s, im_d = re[0] + re[2], re[0] - re[2], im[0] + im[2], im[0] - im[2]
        ro, rp, io, ip = re[1] + re[3], re[1] - re[3], im[1] + im[3], im[1] - im[3]
        pairs = [(rs + ro, im_s + io), (rd + ip, im_d - rp), (rs - ro, im_s - io), (rd - ip, im_d + rp)]
        for r2, (p_re, p_im) in enumerate(pairs):
            work[r2, rows, :128] = p_re.astype(BF)
            work[r2, rows, 128:] = p_im.astype(BF)
    for r2 in range(4):
        spec[r2] = dot(work[r2], fwd_t[r2]).astype(BF)


def inverse_rows(fwd_t, quarter, left):
    for r in range(4):
        turn = lax.rem(quarter * r, 4)
        turn = jnp.full((128, 128), turn, jnp.int32)
        c = fwd_t[r, :128, :128].astype(F32)
        s = fwd_t[r, 128:, :128].astype(F32)
        new_c = jnp.where(turn == 0, c, jnp.where(turn == 1, -s, jnp.where(turn == 2, -c, s))).astype(BF)
        new_s = jnp.where(turn == 0, s, jnp.where(turn == 1, c, jnp.where(turn == 2, -s, -c)))
        left[:128, 256 * r : 256 * r + 128] = new_c
        left[128:, 256 * r + 128 : 256 * r + 256] = new_c
        left[:128, 256 * r + 128 : 256 * r + 256] = (-new_s).astype(BF)
        left[128:, 256 * r : 256 * r + 128] = new_s.astype(BF)


def pair_scores(block, fwd, fwd_t, spec, left, work, prod, best, total, first):
    a0, a1 = [jnp.concatenate([block(q, 0, 0), block(q, 1, 0)], axis=1) for q in range(2)]
    b0, b1 = [jnp.concatenate([block(q, 0, 1), block(q, 1, 1)], axis=1) for q in range(2)]
    stacked = [(a0 + a1, b0 + b1), (a0 + b1, b0 - a1), (a0 - a1, b0 - b1), (a0 - b1, b0 + a1)]
    for r1 in range(4):
        out = dot(fwd[r1], jnp.concatenate(stacked[r1], axis=0)).astype(BF)
        re0, re1, im0, im1 = out[:128, :128], out[:128, 128:], out[128:, :128], out[128:, 128:]
        rows = pl.ds(128 * r1, 128)
        pairs = [(re0 + re1, im0 + im1), (re0 + im1, im0 - re1), (re0 - re1, im0 - im1), (re0 - im1, im0 + re1)]
        for r2, (p_re, p_im) in enumerate(pairs):
            work[r2, rows, :128] = p_re
            work[r2, rows, 128:] = p_im
    for r2 in range(4):
        found = dot(work[r2], fwd_t[r2])
        t_re, t_im = found[:, :128].astype(BF), found[:, 128:].astype(BF)
        x_re, x_im = spec[r2, :, :128], spec[r2, :, 128:]
        p_re = x_re * t_re + x_im * t_im
        p_im = x_im * t_re - x_re * t_im
        lanes = pl.ds(128 * r2, 128)
        for r1 in range(4):
            prod[pl.ds(256 * r1, 128), lanes] = p_re[128 * r1 : 128 * r1 + 128]
            prod[pl.ds(256 * r1 + 128, 128), lanes] = p_im[128 * r1 : 128 * r1 + 128]
    mid = dot(left[...], prod[...]).astype(BF)
    u = []
    for r2 in range(4):
        lanes = slice(128 * r2, 128 * r2 + 128)
        u.append(dot(jnp.concatenate([mid[:128, lanes], mid[128:, lanes]], axis=1), fwd[r2]))
    re = [v[:, :128] for v in u]
    im = [v[:, 128:] for v in u]
    rs, rd, im_s, im_d = re[0] + re[2], re[0] - re[2], im[0] + im[2], im[0] - im[2]
    ro, rp, io, ip = re[1] + re[3], re[1] - re[3], im[1] + im[3], im[1] - im[3]
    one = [rs + ro, rd - ip, rs - ro, rd + ip]
    two = [-(im_s + io), -(im_d + rp), io - im_s, rp - im_d]
    for q in range(4):
        lanes = pl.ds(128 * q, 128)
        top, both = jnp.maximum(one[q], two[q]), one[q] + two[q]
        if first:
            best[:, lanes] = top
            total[:, lanes] = both
        else:
            best[:, lanes] = jnp.maximum(best[:, lanes], top)
            total[:, lanes] = total[:, lanes] + both


def kernel(
    quarter_in, plan_in, mic_in, tmpl_in, fwd_in, fwd_t_in, out,
    quarter, plan, mic, tmpl, fwd, fwd_t, load, turned, got, line, tx, tz, spec, work, prod, left, best, total, give, take,
    a_send, a_recv, y_send, y_recv, sx_send, sx_recv, sz_send, sz_recv, lz_send, lz_recv, bx_send, bx_recv, bz_send, bz_recv, c_send, c_recv,
):
    x, z, y, core = coords()
    early = z < 4
    late = z >= 4
    x_ways = [lax.rem(x + d, 4) for d in (2, 1, 3)]
    x_peers = [device(px, z, y, core) for px in x_ways]
    y_peers = [device(x, z, lax.rem(y + d, 8), core) for d in (4, 3, 5, 2, 6, 1, 7)]
    part = jnp.where(early, z, 7 - z)
    others = [k + (part <= k).astype(jnp.int32) for k in range(3)]
    z_peers = [device(x, jnp.where(early, k, 7 - k), y, core) for k in others]
    partner = device(x, 7 - z, y, core)
    other = device(x, z, y, 1 - core)
    columns = x_ways + [x]

    barrier = pltpu.get_barrier_semaphore()

    def greet(target):
        pl.semaphore_signal(barrier, inc=1, device_id=target, device_id_type=MESH)

    @pl.when(early)
    def _():
        for px in columns:
            for pz in (7, 6, 5, 4, 3, 2, 1, 0):

                @pl.when((px != x) | (z != pz))
                def _():
                    greet(device(px, pz, y, core))

        for target in y_peers:
            greet(target)

    greet(other)
    loads = [
        pltpu.make_async_copy(src, dst, load.at[i])
        for i, (src, dst) in enumerate(
            [(quarter_in, quarter), (tmpl_in, tmpl), (fwd_in, fwd), (mic_in, mic), (fwd_t_in, fwd_t), (plan_in, plan)]
        )
    ]
    for copy in loads:
        copy.start()
    loads[0].wait()
    loads[1].wait()

    block = rotate(tmpl[0, 0], quarter[0, 0])
    for q in range(2):
        for h in range(2):
            chunks = block[128 * q : 128 * q + 128, 128 * h : 128 * h + 128].reshape(4, 2, 16, 128)
            turned[pl.ds(8 * q + 4 * h, 4)] = chunks

    @pl.when(early)
    def _():
        pl.semaphore_wait(barrier, 23)

    @pl.when(late)
    def _():
        pl.semaphore_wait(barrier, 17)

    mine = x * 8 + z

    def scatter(k, pz):
        px = columns[k]
        return remote(
            turned.at[px * 4 + pz], got.at[mine], a_send.at[4 * k + pz], a_recv.at[mine], device(px, pz, y, core)
        )

    for k in range(4):
        for pz in (3, 0, 2, 1):

            @pl.when((z != pz) if k == 3 else (z >= 0))
            def _():
                scatter(k, pz).start()

    for copy in loads[2:]:
        copy.wait()
    tile_spectrum(mic, fwd, fwd_t, work, spec)
    inverse_rows(fwd_t, lax.div(y, 2), left)

    mine_z = pl.ds(2 * part, 2)

    def z_first(p, i):
        ref = tx.at[x, p, mine_z]
        return remote(ref, ref, sz_send.at[p, i], sz_recv.at[p, part], z_peers[i])

    def z_first_from(p, k):
        ref = tx.at[x, p, pl.ds(2 * k, 2)]
        return remote(ref, ref, sz_send.at[p, 0], sz_recv.at[p, k], other)

    def x_first(i):
        ref = tz.at[mine_z, x]
        return remote(ref, ref, sx_send.at[i], sx_recv.at[i], x_peers[i])

    def z_last(i):
        return remote(tz.at[mine_z], tz.at[mine_z], bz_send.at[i], bz_recv.at[part], z_peers[i])

    def z_last_from(k):
        ref = tz.at[pl.ds(2 * k, 2)]
        return remote(ref, ref, bz_send.at[0], bz_recv.at[k], other)

    def across(p):
        ref = tz.at[mine_z, x] if p == 3 else tx.at[x, p, mine_z]
        return remote(ref, ref, lz_send.at[p], lz_recv.at[p], partner)

    def x_last(p, i):
        return remote(tx.at[x, p], tx.at[x, p], bx_send.at[p, i], bx_recv.at[p, i], x_peers[i])

    def to_y(i):
        return remote(line.at[y], line.at[y], y_send.at[i], y_recv.at[y], y_peers[i])

    @pl.when(early)
    def _():
        got[mine] = turned[x * 4 + z]
        for k in range(4):
            for pz in range(8):
                source = columns[k] * 8 + pz

                @pl.when((z != pz) if k == 3 else (z >= 0))
                def _():
                    remote(turned.at[0], got.at[source], a_send.at[0], a_recv.at[source], other).wait_recv()

        owners = [plan[s] for s in range(2)]
        for s in range(2):
            line[y, s] = got[lax.div(owners[s], 2)]
        for i in range(7):
            to_y(i).start()
        odd = [jnp.full((2, 16, 128), lax.rem(owners[s], 2), jnp.int32) for s in range(2)]

        def arrived(pair):
            for low in range(2):
                source = 2 * pair + low

                @pl.when(source != y)
                def _():
                    remote(line.at[source], line.at[source], y_send.at[0], y_recv.at[source], other).wait_recv()

            return [jnp.where(odd[s] == 0, line[2 * pair, s], line[2 * pair + 1, s]) for s in range(2)]

        own = lax.div(y, 2)
        for s, tiles in enumerate(arrived(own)):
            for b in range(2):
                tz[2 * z + b, x, s] = tiles[b]
        for i in range(3):
            x_first(i).start()
        across(3).start()
        for p, pairs in enumerate(((1, 0, 1, 0), (3, 3, 3, 1), (2, 2, 0, 2))):
            chosen = jnp.where(own < 2, jnp.where(own == 0, pairs[0], pairs[1]), jnp.where(own == 2, pairs[2], pairs[3]))
            for s, tiles in enumerate(arrived(chosen)):
                for b in range(2):
                    tx[x, p, 2 * z + b, s] = tiles[b]
            for i in range(3):
                z_first(p, i).start()
            across(p).start()

    @pl.when(late)
    def _():
        across(3).wait_recv()
        for i in range(3):
            x_first(i).start()
        for p in range(3):
            across(p).wait_recv()
            for i in range(3):
                z_first(p, i).start()

    for i in range(3):
        x_first(i).wait_recv()
    for i in range(3):
        z_last(i).start()
    for p in range(3):
        for k in others:
            z_first_from(p, k).wait_recv()
        for i in range(3):
            x_last(p, i).start()

    def from_x(p):
        return lambda q, h, s: tx[2 * q + h, p, :, s].reshape(128, 128)

    def from_z(q, h, s):
        return tz[:, 2 * q + h, s].reshape(128, 128)

    for k in others:
        z_last_from(k).wait_recv()
    pair_scores(from_z, fwd, fwd_t, spec, left, work, prod, best, total, True)
    for i in range(3):
        x_last(0, i).wait_recv()
    pair_scores(from_x(0), fwd, fwd_t, spec, left, work, prod, best, total, False)

    for p in range(1, 3):
        for i in range(3):
            x_last(p, i).wait_recv()
        pair_scores(from_x(p), fwd, fwd_t, spec, left, work, prod, best, total, False)

    theirs, ours = pl.ds((1 - core) * 64, 64), pl.ds(core * 64, 64)
    give[0] = best[theirs, :].astype(BF)
    give[1] = total[theirs, :].astype(BF)
    swap = remote(give, take, c_send, c_recv, other)
    swap.start()
    swap.wait_recv()
    out[0] = jnp.maximum(best[ours, :], take[0].astype(F32))
    out[1] = total[ours, :] + take[1].astype(F32)
    swap.wait_send()
    for k in range(4):
        for pz in range(4):

            @pl.when((z != pz) if k == 3 else (z >= 0))
            def _():
                scatter(k, pz).wait_send()

    for i in range(3):
        x_first(i).wait_send()
        z_last(i).wait_send()
        for p in range(3):
            z_first(p, i).wait_send()
            x_last(p, i).wait_send()

    @pl.when(early)
    def _():
        for i in range(7):
            to_y(i).wait_send()
        for p in range(4):
            across(p).wait_send()


def per_device(micrographs, templates, quarter_turns, plan):
    fwd, fwd_t = radix_tables()
    dma = pltpu.SemaphoreType.DMA
    operands = (quarter_turns, plan, micrographs, templates, jnp.asarray(fwd), jnp.asarray(fwd_t))
    raw = pl.pallas_call(
        kernel,
        out_shape=jax.ShapeDtypeStruct((2, 64, SIDE), F32),
        in_specs=[pl.BlockSpec(memory_space=pltpu.HBM)] * 6,
        out_specs=pl.BlockSpec(memory_space=pltpu.VMEM),
        scratch_shapes=[
            pltpu.SMEM((1, 1), jnp.int32),
            pltpu.SMEM((64,), jnp.int32),
            pltpu.VMEM((1, SIDE, SIDE), BF),
            pltpu.VMEM((1, 1, 256, 256), BF),
            pltpu.VMEM((4, 256, 256), BF),
            pltpu.VMEM((4, 256, 256), BF),
            dma((6,)),
            pltpu.VMEM((16, 2, 16, 128), BF),
            pltpu.VMEM((32, 2, 16, 128), BF),
            pltpu.VMEM((8, 2, 2, 16, 128), BF),
            pltpu.VMEM((4, 3, 8, 2, 16, 128), BF),
            pltpu.VMEM((8, 4, 2, 16, 128), BF),
            pltpu.VMEM((4, 512, 256), BF),
            pltpu.VMEM((4, 512, 256), BF),
            pltpu.VMEM((1024, 512), BF),
            pltpu.VMEM((256, 1024), BF),
            pltpu.VMEM((128, 512), F32),
            pltpu.VMEM((128, 512), F32),
            pltpu.VMEM((2, 64, 512), BF),
            pltpu.VMEM((2, 64, 512), BF),
            dma((16,)), dma((32,)), dma((7,)), dma((8,)), dma((3,)), dma((3,)), dma((3, 3)), dma((3, 4)), dma((4,)), dma((4,)),
            dma((3, 3)), dma((3, 3)), dma((3,)), dma((4,)), dma(()), dma(()),
        ],
        compiler_params=pltpu.CompilerParams(collective_id=0, has_side_effects=True, vmem_limit_bytes=40 << 20),
        name="match",
    )(operands[0], *[pltpu.with_memory_space_constraint(a, pltpu.HBM) for a in operands[1:]])
    scale = 1.0 / (SIDE * SIDE)
    return raw[0:1] * scale, raw[1:2] * (scale / SEARCHED)


def solution(mesh):
    in_specs = (P("tile", None, None), P("tile", "orient", None, None), P("tile", "orient"), P())
    out_specs = (P("tile", "orient", None), P("tile", "orient", None))
    return jax.shard_map(per_device, mesh=mesh, in_specs=in_specs, out_specs=out_specs, check_vma=False)
```

```python
import functools

import jax
import jax.numpy as jnp
import numpy as np
from jax import lax
from jax.experimental import pallas as pl
from jax.experimental.pallas import tpu as pltpu
from jax.sharding import PartitionSpec as P

MESH = pl.DeviceIdType.MESH
BF = jnp.bfloat16
F32 = jnp.float32
SIDE = 512
SEARCHED = 16


def radix_tables():
    j = np.arange(128)
    forward = []
    for r in range(4):
        phase = (np.outer(4 * j + r, j) % SIDE).astype(np.float32)
        angle = np.float32(2.0 * np.pi / SIDE) * phase
        c, s = np.cos(angle), np.sin(angle)
        forward.append(np.block([[c, s], [-s, c]]))
    forward = np.stack(forward).astype(np.float32)
    return forward.astype(jnp.bfloat16), forward.transpose(0, 2, 1).astype(jnp.bfloat16)


def coords():
    tile = lax.axis_index("tile")
    orient = lax.axis_index("orient")
    x, z = lax.div(tile, 16), lax.rem(lax.div(tile, 2), 8)
    y = lax.div(orient, 2) * 2 + lax.rem(tile, 2)
    return x, z, y, lax.rem(orient, 2)


def device(x, z, y, core):
    return (x * 16 + z * 2 + lax.rem(y, 2), lax.div(y, 2) * 2 + core)


def remote(src, dst, send, recv, target):
    return pltpu.make_async_remote_copy(
        src_ref=src, dst_ref=dst, send_sem=send, recv_sem=recv, device_id=target, device_id_type=MESH
    )


def dot(a, b):
    return jnp.dot(a, b, preferred_element_type=F32)


def rotate(block, quarter):
    turns = jnp.full((256, 256), quarter, jnp.int32)
    row = lax.broadcasted_iota(jnp.int32, (256, 256), 0)
    col = lax.broadcasted_iota(jnp.int32, (256, 256), 1)
    same = (row == col).astype(F32)
    swapped = (row + col == 255).astype(F32)
    flip_rows = jnp.where((turns == 1) | (turns == 2), swapped, same).astype(BF)
    flip_cols = jnp.where((turns == 2) | (turns == 3), swapped, same).astype(BF)
    wide = block.astype(F32)
    turned = jnp.where((turns == 1) | (turns == 3), wide.T, wide).astype(BF)
    return dot(dot(flip_rows, turned).astype(BF), flip_cols).astype(BF)


def tile_spectrum(mic, fwd, fwd_t, work, spec):
    quarters = [mic[0, 128 * q : 128 * q + 128, :].astype(F32) for q in range(4)]
    a, b = quarters[0] + quarters[2], quarters[1] + quarters[3]
    c, d = quarters[0] - quarters[2], quarters[1] - quarters[3]
    outs = [
        dot(fwd[0, :, :128], (a + b).astype(BF)),
        dot(fwd[1], jnp.concatenate([c, -d], axis=0).astype(BF)),
        dot(fwd[2, :, :128], (a - b).astype(BF)),
        dot(fwd[3], jnp.concatenate([c, d], axis=0).astype(BF)),
    ]
    for r1 in range(4):
        re = [outs[r1][:128, 128 * p : 128 * p + 128] for p in range(4)]
        im = [outs[r1][128:, 128 * p : 128 * p + 128] for p in range(4)]
        rows = pl.ds(128 * r1, 128)
        rs, rd, im_s, im_d = re[0] + re[2], re[0] - re[2], im[0] + im[2], im[0] - im[2]
        ro, rp, io, ip = re[1] + re[3], re[1] - re[3], im[1] + im[3], im[1] - im[3]
        pairs = [(rs + ro, im_s + io), (rd + ip, im_d - rp), (rs - ro, im_s - io), (rd - ip, im_d + rp)]
        for r2, (p_re, p_im) in enumerate(pairs):
            work[r2, rows, :128] = p_re.astype(BF)
            work[r2, rows, 128:] = p_im.astype(BF)
    for r2 in range(4):
        spec[r2] = dot(work[r2], fwd_t[r2]).astype(BF)


def inverse_rows(fwd_t, quarter, left):
    for r in range(4):
        turn = lax.rem(quarter * r, 4)
        turn = jnp.full((128, 128), turn, jnp.int32)
        c = fwd_t[r, :128, :128].astype(F32)
        s = fwd_t[r, 128:, :128].astype(F32)
        new_c = jnp.where(turn == 0, c, jnp.where(turn == 1, -s, jnp.where(turn == 2, -c, s))).astype(BF)
        new_s = jnp.where(turn == 0, s, jnp.where(turn == 1, c, jnp.where(turn == 2, -s, -c)))
        left[:128, 256 * r : 256 * r + 128] = new_c
        left[128:, 256 * r + 128 : 256 * r + 256] = new_c
        left[:128, 256 * r + 128 : 256 * r + 256] = (-new_s).astype(BF)
        left[128:, 256 * r : 256 * r + 128] = new_s.astype(BF)


def pair_scores(block, fwd, fwd_t, spec, left, work, prod, best, total, first, done=None):
    a0, a1 = [jnp.concatenate([block(q, 0, 0), block(q, 1, 0)], axis=1) for q in range(2)]
    b0, b1 = [jnp.concatenate([block(q, 0, 1), block(q, 1, 1)], axis=1) for q in range(2)]
    stacked = [(a0 + a1, b0 + b1), (a0 + b1, b0 - a1), (a0 - a1, b0 - b1), (a0 - b1, b0 + a1)]
    for r1 in range(4):
        out = dot(fwd[r1], jnp.concatenate(stacked[r1], axis=0)).astype(BF)
        re0, re1, im0, im1 = out[:128, :128], out[:128, 128:], out[128:, :128], out[128:, 128:]
        rows = pl.ds(128 * r1, 128)
        pairs = [(re0 + re1, im0 + im1), (re0 + im1, im0 - re1), (re0 - re1, im0 - im1), (re0 - im1, im0 + re1)]
        for r2, (p_re, p_im) in enumerate(pairs):
            work[r2, rows, :128] = p_re
            work[r2, rows, 128:] = p_im
    for r2 in range(4):
        found = dot(work[r2], fwd_t[r2])
        t_re, t_im = found[:, :128].astype(BF), found[:, 128:].astype(BF)
        x_re, x_im = spec[r2, :, :128], spec[r2, :, 128:]
        p_re = x_re * t_re + x_im * t_im
        p_im = x_im * t_re - x_re * t_im
        lanes = pl.ds(128 * r2, 128)
        for r1 in range(4):
            prod[pl.ds(256 * r1, 128), lanes] = p_re[128 * r1 : 128 * r1 + 128]
            prod[pl.ds(256 * r1 + 128, 128), lanes] = p_im[128 * r1 : 128 * r1 + 128]
    mid = dot(left[...], prod[...]).astype(BF)
    u = []
    for r2 in range(4):
        lanes = slice(128 * r2, 128 * r2 + 128)
        u.append(dot(jnp.concatenate([mid[:128, lanes], mid[128:, lanes]], axis=1), fwd[r2]))
    re = [v[:, :128] for v in u]
    im = [v[:, 128:] for v in u]
    rs, rd, im_s, im_d = re[0] + re[2], re[0] - re[2], im[0] + im[2], im[0] - im[2]
    ro, rp, io, ip = re[1] + re[3], re[1] - re[3], im[1] + im[3], im[1] - im[3]
    one = [rs + ro, rd - ip, rs - ro, rd + ip]
    two = [-(im_s + io), -(im_d + rp), io - im_s, rp - im_d]
    for q in range(4):
        lanes = pl.ds(128 * q, 128)
        top, both = jnp.maximum(one[q], two[q]), one[q] + two[q]
        if first:
            best[:, lanes] = top
            total[:, lanes] = both
        else:
            best[:, lanes] = jnp.maximum(best[:, lanes], top)
            total[:, lanes] = total[:, lanes] + both
        if done is not None:
            done(q)


def kernel(
    quarter_in, plan_in, mic_in, tmpl_in, fwd_in, fwd_t_in, out,
    quarter, plan, mic, tmpl, fwd, fwd_t, load, turned, got, line, tx, tz, spec, work, prod, left, best, total, give, take,
    a_send, a_recv, y_send, y_recv, sx_send, sx_recv, sz_send, sz_recv, lz_send, lz_recv, bx_send, bx_recv, bz_send, bz_recv, c_send, c_recv,
):
    x, z, y, core = coords()
    early = z < 4
    late = z >= 4
    x_ways = [lax.rem(x + d, 4) for d in (2, 1, 3)]
    x_peers = [device(px, z, y, core) for px in x_ways]
    y_peers = [device(x, z, lax.rem(y + d, 8), core) for d in (4, 3, 5, 2, 6, 1, 7)]
    part = jnp.where(early, z, 7 - z)
    mirrored = jnp.where(early, part, 3 - part)
    others = [k + (mirrored <= k).astype(jnp.int32) for k in range(3)]
    others = [jnp.where(early, k, 3 - k) for k in others]
    z_peers = [device(x, jnp.where(early, k, 7 - k), y, core) for k in others]
    partner = device(x, 7 - z, y, core)
    other = device(x, z, y, 1 - core)
    columns = x_ways + [x]

    barrier = pltpu.get_barrier_semaphore()

    def greet(target):
        pl.semaphore_signal(barrier, inc=1, device_id=target, device_id_type=MESH)

    @pl.when(early)
    def _():
        for px in columns:
            for pz in (7, 6, 5, 4, 3, 2, 1, 0):

                @pl.when((px != x) | (z != pz))
                def _():
                    greet(device(px, pz, y, core))

        for target in y_peers:
            greet(target)

    greet(other)
    loads = [
        pltpu.make_async_copy(src, dst, load.at[i])
        for i, (src, dst) in enumerate(
            [(quarter_in, quarter), (tmpl_in, tmpl), (fwd_in, fwd), (mic_in, mic), (fwd_t_in, fwd_t), (plan_in, plan)]
        )
    ]
    for copy in loads:
        copy.start()
    loads[0].wait()
    loads[1].wait()

    block = rotate(tmpl[0, 0], quarter[0, 0])
    for q in range(2):
        for h in range(2):
            chunks = block[128 * q : 128 * q + 128, 128 * h : 128 * h + 128].reshape(4, 2, 16, 128)
            turned[pl.ds(8 * q + 4 * h, 4)] = chunks

    @pl.when(early)
    def _():
        pl.semaphore_wait(barrier, 23)

    @pl.when(late)
    def _():
        pl.semaphore_wait(barrier, 17)

    mine = x * 8 + z

    def scatter(k, pz):
        px = columns[k]
        return remote(
            turned.at[px * 4 + pz], got.at[mine], a_send.at[4 * k + pz], a_recv.at[mine], device(px, pz, y, core)
        )

    for k in range(4):
        for pz in (3, 0, 2, 1):

            @pl.when((z != pz) if k == 3 else (z >= 0))
            def _():
                scatter(k, pz).start()

    for copy in loads[2:]:
        copy.wait()
    tile_spectrum(mic, fwd, fwd_t, work, spec)
    inverse_rows(fwd_t, lax.div(y, 2), left)

    mine_z = pl.ds(2 * part, 2)

    def z_first(p, i):
        ref = tx.at[x, p, mine_z]
        return remote(ref, ref, sz_send.at[p, i], sz_recv.at[p, part], z_peers[i])

    def z_first_from(p, k):
        ref = tx.at[x, p, pl.ds(2 * k, 2)]
        return remote(ref, ref, sz_send.at[p, 0], sz_recv.at[p, k], other)

    def x_first(i):
        ref = tz.at[mine_z, x]
        return remote(ref, ref, sx_send.at[i], sx_recv.at[i], x_peers[i])

    def z_last(i):
        return remote(tz.at[mine_z], tz.at[mine_z], bz_send.at[i], bz_recv.at[part], z_peers[i])

    def z_last_from(k):
        ref = tz.at[pl.ds(2 * k, 2)]
        return remote(ref, ref, bz_send.at[0], bz_recv.at[k], other)

    def across(p):
        ref = tz.at[mine_z, x] if p == 3 else tx.at[x, p, mine_z]
        return remote(ref, ref, lz_send.at[p], lz_recv.at[p], partner)

    def x_last(p, i):
        return remote(tx.at[x, p], tx.at[x, p], bx_send.at[p, i], bx_recv.at[p, i], x_peers[i])

    def to_y(i):
        return remote(line.at[y], line.at[y], y_send.at[i], y_recv.at[y], y_peers[i])

    @pl.when(early)
    def _():
        got[mine] = turned[x * 4 + z]
        for k in range(4):
            for pz in range(8):
                source = columns[k] * 8 + pz

                @pl.when((z != pz) if k == 3 else (z >= 0))
                def _():
                    remote(turned.at[0], got.at[source], a_send.at[0], a_recv.at[source], other).wait_recv()

        owners = [plan[s] for s in range(2)]
        for s in range(2):
            line[y, s] = got[lax.div(owners[s], 2)]
        for i in range(7):
            to_y(i).start()
        odd = [jnp.full((2, 16, 128), lax.rem(owners[s], 2), jnp.int32) for s in range(2)]

        def arrived(pair):
            for low in range(2):
                source = 2 * pair + low

                @pl.when(source != y)
                def _():
                    remote(line.at[source], line.at[source], y_send.at[0], y_recv.at[source], other).wait_recv()

            return [jnp.where(odd[s] == 0, line[2 * pair, s], line[2 * pair + 1, s]) for s in range(2)]

        own = lax.div(y, 2)
        for s, tiles in enumerate(arrived(own)):
            for b in range(2):
                tz[2 * z + b, x, s] = tiles[b]
        across(3).start()
        for i in range(3):
            x_first(i).start()
        for p, pairs in enumerate(((1, 0, 1, 0), (3, 3, 3, 1), (2, 2, 0, 2))):
            chosen = jnp.where(own < 2, jnp.where(own == 0, pairs[0], pairs[1]), jnp.where(own == 2, pairs[2], pairs[3]))
            for s, tiles in enumerate(arrived(chosen)):
                for b in range(2):
                    tx[x, p, 2 * z + b, s] = tiles[b]
            across(p).start()
            for i in range(3):
                z_first(p, i).start()

    @pl.when(late)
    def _():
        across(3).wait_recv()
        for i in range(3):
            x_first(i).start()
        for p in range(3):
            across(p).wait_recv()
            for i in range(3):
                z_first(p, i).start()

    for i in range(3):
        x_first(i).wait_recv()
    for i in range(3):
        z_last(i).start()
    for p in range(3):
        for k in others:
            z_first_from(p, k).wait_recv()
        for i in range(3):
            x_last(p, i).start()

    def from_x(p):
        return lambda q, h, s: tx[2 * q + h, p, :, s].reshape(128, 128)

    def from_z(q, h, s):
        return tz[:, 2 * q + h, s].reshape(128, 128)

    for k in others:
        z_last_from(k).wait_recv()
    pair_scores(from_z, fwd, fwd_t, spec, left, work, prod, best, total, True)
    for i in range(3):
        x_last(0, i).wait_recv()
    pair_scores(from_x(0), fwd, fwd_t, spec, left, work, prod, best, total, False)

    theirs, ours = pl.ds((1 - core) * 64, 64), pl.ds(core * 64, 64)

    def swap(q):
        return remote(give.at[q], take.at[q], c_send.at[q], c_recv.at[q], other)

    def hand_over(q):
        lanes = pl.ds(128 * q, 128)
        give[q, 0] = best[theirs, lanes].astype(BF)
        give[q, 1] = total[theirs, lanes].astype(BF)
        swap(q).start()

    for p in range(1, 3):
        for i in range(3):
            x_last(p, i).wait_recv()
        done = hand_over if p == 2 else None
        pair_scores(from_x(p), fwd, fwd_t, spec, left, work, prod, best, total, False, done)
    for q in range(4):
        lanes = pl.ds(128 * q, 128)
        swap(q).wait_recv()
        out[0, :, lanes] = jnp.maximum(best[ours, lanes], take[q, 0].astype(F32))
        out[1, :, lanes] = total[ours, lanes] + take[q, 1].astype(F32)
    for q in range(4):
        swap(q).wait_send()
    for k in range(4):
        for pz in range(4):

            @pl.when((z != pz) if k == 3 else (z >= 0))
            def _():
                scatter(k, pz).wait_send()

    for i in range(3):
        x_first(i).wait_send()
        z_last(i).wait_send()
        for p in range(3):
            z_first(p, i).wait_send()
            x_last(p, i).wait_send()

    @pl.when(early)
    def _():
        for i in range(7):
            to_y(i).wait_send()
        for p in range(4):
            across(p).wait_send()


def per_device(micrographs, templates, quarter_turns, plan):
    fwd, fwd_t = radix_tables()
    dma = pltpu.SemaphoreType.DMA
    operands = (quarter_turns, plan, micrographs, templates, jnp.asarray(fwd), jnp.asarray(fwd_t))
    raw = pl.pallas_call(
        kernel,
        out_shape=jax.ShapeDtypeStruct((2, 64, SIDE), F32),
        in_specs=[pl.BlockSpec(memory_space=pltpu.HBM)] * 6,
        out_specs=pl.BlockSpec(memory_space=pltpu.VMEM),
        scratch_shapes=[
            pltpu.SMEM((1, 1), jnp.int32),
            pltpu.SMEM((64,), jnp.int32),
            pltpu.VMEM((1, SIDE, SIDE), BF),
            pltpu.VMEM((1, 1, 256, 256), BF),
            pltpu.VMEM((4, 256, 256), BF),
            pltpu.VMEM((4, 256, 256), BF),
            dma((6,)),
            pltpu.VMEM((16, 2, 16, 128), BF),
            pltpu.VMEM((32, 2, 16, 128), BF),
            pltpu.VMEM((8, 2, 2, 16, 128), BF),
            pltpu.VMEM((4, 3, 8, 2, 16, 128), BF),
            pltpu.VMEM((8, 4, 2, 16, 128), BF),
            pltpu.VMEM((4, 512, 256), BF),
            pltpu.VMEM((4, 512, 256), BF),
            pltpu.VMEM((1024, 512), BF),
            pltpu.VMEM((256, 1024), BF),
            pltpu.VMEM((128, 512), F32),
            pltpu.VMEM((128, 512), F32),
            pltpu.VMEM((4, 2, 64, 128), BF),
            pltpu.VMEM((4, 2, 64, 128), BF),
            dma((16,)), dma((32,)), dma((7,)), dma((8,)), dma((3,)), dma((3,)), dma((3, 3)), dma((3, 4)), dma((4,)), dma((4,)),
            dma((3, 3)), dma((3, 3)), dma((3,)), dma((4,)), dma((4,)), dma((4,)),
        ],
        compiler_params=pltpu.CompilerParams(collective_id=0, has_side_effects=True, vmem_limit_bytes=40 << 20),
        name="match",
    )(operands[0], *[pltpu.with_memory_space_constraint(a, pltpu.HBM) for a in operands[1:]])
    scale = 1.0 / (SIDE * SIDE)
    return raw[0:1] * scale, raw[1:2] * (scale / SEARCHED)


def solution(mesh):
    in_specs = (P("tile", None, None), P("tile", "orient", None, None), P("tile", "orient"), P())
    out_specs = (P("tile", "orient", None), P("tile", "orient", None))
    return jax.shard_map(per_device, mesh=mesh, in_specs=in_specs, out_specs=out_specs, check_vma=False)
```

```python
import functools

import jax
import jax.numpy as jnp
import numpy as np
from jax import lax
from jax.experimental import pallas as pl
from jax.experimental.pallas import tpu as pltpu
from jax.sharding import PartitionSpec as P

MESH = pl.DeviceIdType.MESH
BF = jnp.bfloat16
F32 = jnp.float32
SIDE = 512
SEARCHED = 16


def radix_tables():
    j = np.arange(128)
    forward = []
    for r in range(4):
        phase = (np.outer(4 * j + r, j) % SIDE).astype(np.float32)
        angle = np.float32(2.0 * np.pi / SIDE) * phase
        c, s = np.cos(angle), np.sin(angle)
        forward.append(np.block([[c, s], [-s, c]]))
    forward = np.stack(forward).astype(np.float32)
    return forward.astype(jnp.bfloat16), forward.transpose(0, 2, 1).astype(jnp.bfloat16)


def coords():
    tile = lax.axis_index("tile")
    orient = lax.axis_index("orient")
    x, z = lax.div(tile, 16), lax.rem(lax.div(tile, 2), 8)
    y = lax.div(orient, 2) * 2 + lax.rem(tile, 2)
    return x, z, y, lax.rem(orient, 2)


def device(x, z, y, core):
    return (x * 16 + z * 2 + lax.rem(y, 2), lax.div(y, 2) * 2 + core)


def remote(src, dst, send, recv, target):
    return pltpu.make_async_remote_copy(
        src_ref=src, dst_ref=dst, send_sem=send, recv_sem=recv, device_id=target, device_id_type=MESH
    )


def dot(a, b):
    return jnp.dot(a, b, preferred_element_type=F32)


def rotate(block, quarter):
    turns = jnp.full((256, 256), quarter, jnp.int32)
    row = lax.broadcasted_iota(jnp.int32, (256, 256), 0)
    col = lax.broadcasted_iota(jnp.int32, (256, 256), 1)
    same = (row == col).astype(F32)
    swapped = (row + col == 255).astype(F32)
    flip_rows = jnp.where((turns == 1) | (turns == 2), swapped, same).astype(BF)
    flip_cols = jnp.where((turns == 2) | (turns == 3), swapped, same).astype(BF)
    wide = block.astype(F32)
    turned = jnp.where((turns == 1) | (turns == 3), wide.T, wide).astype(BF)
    return dot(dot(flip_rows, turned).astype(BF), flip_cols).astype(BF)


def tile_spectrum(mic, fwd, fwd_t, work, spec):
    quarters = [mic[0, 128 * q : 128 * q + 128, :].astype(F32) for q in range(4)]
    a, b = quarters[0] + quarters[2], quarters[1] + quarters[3]
    c, d = quarters[0] - quarters[2], quarters[1] - quarters[3]
    outs = [
        dot(fwd[0, :, :128], (a + b).astype(BF)),
        dot(fwd[1], jnp.concatenate([c, -d], axis=0).astype(BF)),
        dot(fwd[2, :, :128], (a - b).astype(BF)),
        dot(fwd[3], jnp.concatenate([c, d], axis=0).astype(BF)),
    ]
    for r1 in range(4):
        re = [outs[r1][:128, 128 * p : 128 * p + 128] for p in range(4)]
        im = [outs[r1][128:, 128 * p : 128 * p + 128] for p in range(4)]
        rows = pl.ds(128 * r1, 128)
        rs, rd, im_s, im_d = re[0] + re[2], re[0] - re[2], im[0] + im[2], im[0] - im[2]
        ro, rp, io, ip = re[1] + re[3], re[1] - re[3], im[1] + im[3], im[1] - im[3]
        pairs = [(rs + ro, im_s + io), (rd + ip, im_d - rp), (rs - ro, im_s - io), (rd - ip, im_d + rp)]
        for r2, (p_re, p_im) in enumerate(pairs):
            work[r2, rows, :128] = p_re.astype(BF)
            work[r2, rows, 128:] = p_im.astype(BF)
    for r2 in range(4):
        spec[r2] = dot(work[r2], fwd_t[r2]).astype(BF)


def inverse_rows(fwd_t, quarter, left):
    for r in range(4):
        turn = lax.rem(quarter * r, 4)
        turn = jnp.full((128, 128), turn, jnp.int32)
        c = fwd_t[r, :128, :128].astype(F32)
        s = fwd_t[r, 128:, :128].astype(F32)
        new_c = jnp.where(turn == 0, c, jnp.where(turn == 1, -s, jnp.where(turn == 2, -c, s))).astype(BF)
        new_s = jnp.where(turn == 0, s, jnp.where(turn == 1, c, jnp.where(turn == 2, -s, -c)))
        left[:128, 256 * r : 256 * r + 128] = new_c
        left[128:, 256 * r + 128 : 256 * r + 256] = new_c
        left[:128, 256 * r + 128 : 256 * r + 256] = (-new_s).astype(BF)
        left[128:, 256 * r : 256 * r + 128] = new_s.astype(BF)


def pair_scores(block, fwd, fwd_t, spec, left, work, prod, best, total, first):
    a0, a1 = [jnp.concatenate([block(q, 0, 0), block(q, 1, 0)], axis=1) for q in range(2)]
    b0, b1 = [jnp.concatenate([block(q, 0, 1), block(q, 1, 1)], axis=1) for q in range(2)]
    stacked = [(a0 + a1, b0 + b1), (a0 + b1, b0 - a1), (a0 - a1, b0 - b1), (a0 - b1, b0 + a1)]
    for r1 in range(4):
        out = dot(fwd[r1], jnp.concatenate(stacked[r1], axis=0)).astype(BF)
        re0, re1, im0, im1 = out[:128, :128], out[:128, 128:], out[128:, :128], out[128:, 128:]
        rows = pl.ds(128 * r1, 128)
        pairs = [(re0 + re1, im0 + im1), (re0 + im1, im0 - re1), (re0 - re1, im0 - im1), (re0 - im1, im0 + re1)]
        for r2, (p_re, p_im) in enumerate(pairs):
            work[r2, rows, :128] = p_re
            work[r2, rows, 128:] = p_im
    for r2 in range(4):
        found = dot(work[r2], fwd_t[r2])
        t_re, t_im = found[:, :128].astype(BF), found[:, 128:].astype(BF)
        x_re, x_im = spec[r2, :, :128], spec[r2, :, 128:]
        p_re = x_re * t_re + x_im * t_im
        p_im = x_im * t_re - x_re * t_im
        lanes = pl.ds(128 * r2, 128)
        for r1 in range(4):
            prod[pl.ds(256 * r1, 128), lanes] = p_re[128 * r1 : 128 * r1 + 128]
            prod[pl.ds(256 * r1 + 128, 128), lanes] = p_im[128 * r1 : 128 * r1 + 128]
    mid = dot(left[...], prod[...]).astype(BF)
    u = []
    for r2 in range(4):
        lanes = slice(128 * r2, 128 * r2 + 128)
        u.append(dot(jnp.concatenate([mid[:128, lanes], mid[128:, lanes]], axis=1), fwd[r2]))
    re = [v[:, :128] for v in u]
    im = [v[:, 128:] for v in u]
    rs, rd, im_s, im_d = re[0] + re[2], re[0] - re[2], im[0] + im[2], im[0] - im[2]
    ro, rp, io, ip = re[1] + re[3], re[1] - re[3], im[1] + im[3], im[1] - im[3]
    one = [rs + ro, rd - ip, rs - ro, rd + ip]
    two = [-(im_s + io), -(im_d + rp), io - im_s, rp - im_d]
    for q in range(4):
        lanes = pl.ds(128 * q, 128)
        top, both = jnp.maximum(one[q], two[q]), one[q] + two[q]
        if first:
            best[:, lanes] = top
            total[:, lanes] = both
        else:
            best[:, lanes] = jnp.maximum(best[:, lanes], top)
            total[:, lanes] = total[:, lanes] + both


def kernel(
    quarter_in, plan_in, mic_in, tmpl_in, fwd_in, fwd_t_in, out,
    quarter, plan, mic, tmpl, fwd, fwd_t, load, turned, got, line, tx, tz, spec, work, prod, left, best, total, give, take,
    a_send, a_recv, y_send, y_recv, sx_send, sx_recv, sz_send, sz_recv, lz_send, lz_recv, bx_send, bx_recv, bz_send, bz_recv, c_send, c_recv,
):
    x, z, y, core = coords()
    early = z < 4
    late = z >= 4
    x_ways = [lax.rem(x + d, 4) for d in (2, 1, 3)]
    x_peers = [device(px, z, y, core) for px in x_ways]
    y_peers = [device(x, z, lax.rem(y + d, 8), core) for d in (4, 3, 5, 2, 6, 1, 7)]
    part = jnp.where(early, z, 7 - z)
    others = [k + (part <= k).astype(jnp.int32) for k in range(3)]
    z_peers = [device(x, jnp.where(early, k, 7 - k), y, core) for k in others]
    partner = device(x, 7 - z, y, core)
    other = device(x, z, y, 1 - core)
    columns = x_ways + [x]

    barrier = pltpu.get_barrier_semaphore()

    def greet(target):
        pl.semaphore_signal(barrier, inc=1, device_id=target, device_id_type=MESH)

    @pl.when(early)
    def _():
        for px in columns:
            for pz in range(4):

                @pl.when((px != x) | (z != pz))
                def _():
                    greet(device(px, pz, y, core))

        for target in y_peers:
            greet(target)
        for px in columns:
            for pz in range(4, 8):
                greet(device(px, pz, y, core))

    greet(other)
    loads = [
        pltpu.make_async_copy(src, dst, load.at[i])
        for i, (src, dst) in enumerate(
            [(quarter_in, quarter), (tmpl_in, tmpl), (fwd_in, fwd), (mic_in, mic), (fwd_t_in, fwd_t), (plan_in, plan)]
        )
    ]
    for copy in loads:
        copy.start()
    loads[0].wait()
    loads[1].wait()

    block = rotate(tmpl[0, 0], quarter[0, 0])
    for q in range(2):
        for h in range(2):
            chunks = block[128 * q : 128 * q + 128, 128 * h : 128 * h + 128].reshape(4, 2, 16, 128)
            turned[pl.ds(8 * q + 4 * h, 4)] = chunks

    @pl.when(early)
    def _():
        pl.semaphore_wait(barrier, 23)

    @pl.when(late)
    def _():
        pl.semaphore_wait(barrier, 17)

    mine = x * 8 + z

    def scatter(k, pz):
        px = columns[k]
        return remote(
            turned.at[px * 4 + pz], got.at[mine], a_send.at[4 * k + pz], a_recv.at[mine], device(px, pz, y, core)
        )

    for k in range(4):
        for pz in (3, 0, 2, 1):

            @pl.when((z != pz) if k == 3 else (z >= 0))
            def _():
                scatter(k, pz).start()

    for copy in loads[2:]:
        copy.wait()
    tile_spectrum(mic, fwd, fwd_t, work, spec)
    inverse_rows(fwd_t, lax.div(y, 2), left)

    mine_z = pl.ds(2 * part, 2)

    def z_first(p, i):
        ref = tx.at[x, p, mine_z]
        return remote(ref, ref, sz_send.at[p, i], sz_recv.at[p, part], z_peers[i])

    def z_first_from(p, k):
        ref = tx.at[x, p, pl.ds(2 * k, 2)]
        return remote(ref, ref, sz_send.at[p, 0], sz_recv.at[p, k], other)

    def x_first(i):
        ref = tz.at[mine_z, x]
        return remote(ref, ref, sx_send.at[i], sx_recv.at[i], x_peers[i])

    def z_last(i):
        return remote(tz.at[mine_z], tz.at[mine_z], bz_send.at[i], bz_recv.at[part], z_peers[i])

    def z_last_from(k):
        ref = tz.at[pl.ds(2 * k, 2)]
        return remote(ref, ref, bz_send.at[0], bz_recv.at[k], other)

    def across(p):
        ref = tz.at[mine_z, x] if p == 3 else tx.at[x, p, mine_z]
        return remote(ref, ref, lz_send.at[p], lz_recv.at[p], partner)

    def x_last(p, i):
        return remote(tx.at[x, p], tx.at[x, p], bx_send.at[p, i], bx_recv.at[p, i], x_peers[i])

    def to_y(i):
        return remote(line.at[y], line.at[y], y_send.at[i], y_recv.at[y], y_peers[i])

    @pl.when(early)
    def _():
        got[mine] = turned[x * 4 + z]
        for k in range(4):
            for pz in range(8):
                source = columns[k] * 8 + pz

                @pl.when((z != pz) if k == 3 else (z >= 0))
                def _():
                    remote(turned.at[0], got.at[source], a_send.at[0], a_recv.at[source], other).wait_recv()

        owners = [plan[s] for s in range(2)]
        for s in range(2):
            line[y, s] = got[lax.div(owners[s], 2)]
        for i in range(7):
            to_y(i).start()
        odd = [jnp.full((2, 16, 128), lax.rem(owners[s], 2), jnp.int32) for s in range(2)]

        def arrived(pair):
            for low in range(2):
                source = 2 * pair + low

                @pl.when(source != y)
                def _():
                    remote(line.at[source], line.at[source], y_send.at[0], y_recv.at[source], other).wait_recv()

            return [jnp.where(odd[s] == 0, line[2 * pair, s], line[2 * pair + 1, s]) for s in range(2)]

        own = lax.div(y, 2)
        for s, tiles in enumerate(arrived(own)):
            for b in range(2):
                tz[2 * z + b, x, s] = tiles[b]
        for i in range(3):
            x_first(i).start()
        across(3).start()
        for p, pairs in enumerate(((1, 0, 1, 0), (3, 3, 3, 1), (2, 2, 0, 2))):
            chosen = jnp.where(own < 2, jnp.where(own == 0, pairs[0], pairs[1]), jnp.where(own == 2, pairs[2], pairs[3]))
            for s, tiles in enumerate(arrived(chosen)):
                for b in range(2):
                    tx[x, p, 2 * z + b, s] = tiles[b]
            for i in range(3):
                z_first(p, i).start()
            across(p).start()

    @pl.when(late)
    def _():
        across(3).wait_recv()
        for i in range(3):
            x_first(i).start()
        for p in range(3):
            across(p).wait_recv()
            for i in range(3):
                z_first(p, i).start()

    for i in range(3):
        x_first(i).wait_recv()
    for i in range(3):
        z_last(i).start()
    for p in range(3):
        for k in others:
            z_first_from(p, k).wait_recv()
        for i in range(3):
            x_last(p, i).start()

    def from_x(p):
        return lambda q, h, s: tx[2 * q + h, p, :, s].reshape(128, 128)

    def from_z(q, h, s):
        return tz[:, 2 * q + h, s].reshape(128, 128)

    for k in others:
        z_last_from(k).wait_recv()
    pair_scores(from_z, fwd, fwd_t, spec, left, work, prod, best, total, True)
    for i in range(3):
        x_last(0, i).wait_recv()
    pair_scores(from_x(0), fwd, fwd_t, spec, left, work, prod, best, total, False)

    for p in range(1, 3):
        for i in range(3):
            x_last(p, i).wait_recv()
        pair_scores(from_x(p), fwd, fwd_t, spec, left, work, prod, best, total, False)

    theirs, ours = pl.ds((1 - core) * 64, 64), pl.ds(core * 64, 64)
    give[0] = best[theirs, :].astype(BF)
    give[1] = total[theirs, :].astype(BF)
    swap = remote(give, take, c_send, c_recv, other)
    swap.start()
    swap.wait_recv()
    out[0] = jnp.maximum(best[ours, :], take[0].astype(F32))
    out[1] = total[ours, :] + take[1].astype(F32)
    swap.wait_send()
    for k in range(4):
        for pz in range(4):

            @pl.when((z != pz) if k == 3 else (z >= 0))
            def _():
                scatter(k, pz).wait_send()

    for i in range(3):
        x_first(i).wait_send()
        z_last(i).wait_send()
        for p in range(3):
            z_first(p, i).wait_send()
            x_last(p, i).wait_send()

    @pl.when(early)
    def _():
        for i in range(7):
            to_y(i).wait_send()
        for p in range(4):
            across(p).wait_send()


def per_device(micrographs, templates, quarter_turns, plan):
    fwd, fwd_t = radix_tables()
    dma = pltpu.SemaphoreType.DMA
    operands = (quarter_turns, plan, micrographs, templates, jnp.asarray(fwd), jnp.asarray(fwd_t))
    raw = pl.pallas_call(
        kernel,
        out_shape=jax.ShapeDtypeStruct((2, 64, SIDE), F32),
        in_specs=[pl.BlockSpec(memory_space=pltpu.HBM)] * 6,
        out_specs=pl.BlockSpec(memory_space=pltpu.VMEM),
        scratch_shapes=[
            pltpu.SMEM((1, 1), jnp.int32),
            pltpu.SMEM((64,), jnp.int32),
            pltpu.VMEM((1, SIDE, SIDE), BF),
            pltpu.VMEM((1, 1, 256, 256), BF),
            pltpu.VMEM((4, 256, 256), BF),
            pltpu.VMEM((4, 256, 256), BF),
            dma((6,)),
            pltpu.VMEM((16, 2, 16, 128), BF),
            pltpu.VMEM((32, 2, 16, 128), BF),
            pltpu.VMEM((8, 2, 2, 16, 128), BF),
            pltpu.VMEM((4, 3, 8, 2, 16, 128), BF),
            pltpu.VMEM((8, 4, 2, 16, 128), BF),
            pltpu.VMEM((4, 512, 256), BF),
            pltpu.VMEM((4, 512, 256), BF),
            pltpu.VMEM((1024, 512), BF),
            pltpu.VMEM((256, 1024), BF),
            pltpu.VMEM((128, 512), F32),
            pltpu.VMEM((128, 512), F32),
            pltpu.VMEM((2, 64, 512), BF),
            pltpu.VMEM((2, 64, 512), BF),
            dma((16,)), dma((32,)), dma((7,)), dma((8,)), dma((3,)), dma((3,)), dma((3, 3)), dma((3, 4)), dma((4,)), dma((4,)),
            dma((3, 3)), dma((3, 3)), dma((3,)), dma((4,)), dma(()), dma(()),
        ],
        compiler_params=pltpu.CompilerParams(collective_id=0, has_side_effects=True, vmem_limit_bytes=40 << 20),
        name="match",
    )(operands[0], *[pltpu.with_memory_space_constraint(a, pltpu.HBM) for a in operands[1:]])
    scale = 1.0 / (SIDE * SIDE)
    return raw[0:1] * scale, raw[1:2] * (scale / SEARCHED)


def solution(mesh):
    in_specs = (P("tile", None, None), P("tile", "orient", None, None), P("tile", "orient"), P())
    out_specs = (P("tile", "orient", None), P("tile", "orient", None))
    return jax.shard_map(per_device, mesh=mesh, in_specs=in_specs, out_specs=out_specs, check_vma=False)
```
